512 devices in a mesh: dp: 32 (over z, core), expert: 16 (over x, y).
Axes of the slice: x: 4, y: 4, z: 16, core: 2. Of those that a mesh axis runs over, the one named last changes fastest.
Arguments:
- tokens: bfloat16 [65536, 2048], P(('dp', 'expert'))
- targets: bfloat16 [65536, 2048], P(('dp', 'expert'))
- routes: int32 [65536, 8], P(('dp', 'expert')), may hold values from 0 to 15, all different within a row; in each aligned block of 128 rows (0 to 127, 128 to 255, ...) at most 64 rows name the same one
- route_logits: float32 [65536, 8], P(('dp', 'expert')), may hold values from -3 to 3
- slot_order: int32 [65536, 8], P(('dp', 'expert')), may hold values from 0 to 7, each once within a row
- seq_ids: int32 [65536], P(('dp', 'expert')), may hold values from 0 to 63, as said below
- w_gate: bfloat16 [16, 2048, 384], P('expert')
- w_up: bfloat16 [16, 2048, 384], P('expert')
- w_down: bfloat16 [2048, 16, 384], P('dp', 'expert')
Outputs:
- mixed: bfloat16 [65536, 2048], P(('dp', 'expert'))
- seq_loss: float32 [64], replicated
- dual_weight: float32 [64], replicated
- grad_down: float32 [2048, 16, 384], P('dp', 'expert')
The draws below stay inside these ranges and needn't reach their ends.
Inputs may be any that keep to these rules, and one draw needn't show every extreme that they name: `routes`: in each aligned block of 128 rows (the rows of one device) every expert is named by exactly 64 rows; the 8 numbers of a row differ. `slot_order`: each row is a permutation of 0 to 7. `seq_ids`: sequence numbers never fall along the tokens, and every number names one or more tokens.
All inputs are finite; a program needn't handle non-finite values.
Results may differ from the reference program's by a relative error of at most 0.0046.
Values may be sent and summed in bfloat16 or wider, within the bound.
A program may use at most 64 MiB of HBM per device.

```python
import math
import jax
import jax.numpy as jnp
import numpy as np
from jax import lax

D = 2048
H = 384
EXPERTS = 16
TOP = 8
NSEQ = 64
BISECT_STEPS = 40
TOK_DEV = 128
TOKENS = 65536
CAP = 64
GRAD_SCALE = 8192


shared_part = 0.9


own_part = 0.4359


def sequence_numbers(key):
    span = TOKENS // NSEQ
    reach = max(span // 4, 1)
    shifts = jax.random.randint(jax.random.fold_in(key, 7), (NSEQ - 1,), 0, reach + 1)
    bounds = jnp.arange(1, NSEQ, dtype=jnp.int32) * span + shifts.astype(jnp.int32)
    positions = jnp.arange(TOKENS, dtype=jnp.int32)
    return jnp.sum((positions[:, None] >= bounds[None, :]).astype(jnp.int32), axis=1).astype(jnp.int32)


def blended(key, full_shape, common_shape, fan_in):
    common = jax.random.normal(jax.random.fold_in(key, 1), common_shape, jnp.float32)
    own = jax.random.normal(jax.random.fold_in(key, 2), full_shape, jnp.float32)
    mixture = jnp.clip(shared_part * common + own_part * own, -6.0, 6.0)
    return (mixture * float(fan_in) ** (-0.5)).astype(jnp.bfloat16)


def draw_seq_ids(key, part):
    return sequence_numbers(key)


def draw_tokens(key, part):
    seq_number = sequence_numbers(key)
    key = jax.random.fold_in(key, 19)
    scales = jnp.exp(jax.random.uniform(jax.random.fold_in(key, 1), (NSEQ,), jnp.float32, -0.35, 0.35))
    noise = jnp.clip(jax.random.normal(jax.random.fold_in(key, 2), (TOKENS, D), jnp.float32), -6.0, 6.0)
    return (noise * scales[seq_number][:, None]).astype(jnp.bfloat16)


def draw_targets(key, part):
    seq_number = sequence_numbers(key)
    key = jax.random.fold_in(key, 23)
    levels = 0.7 * jnp.exp(jax.random.uniform(jax.random.fold_in(key, 11), (NSEQ,), jnp.float32, -0.7, 0.7))
    noise = jax.random.normal(jax.random.fold_in(key, 13), (TOKENS, D), jnp.float32)
    return (noise * levels[seq_number][:, None]).astype(jnp.bfloat16)


def draw_w_gate(key, part):
    key = jax.random.fold_in(key, 29)
    return blended(key, (EXPERTS, D, H), (1, D, H), D)


def draw_w_up(key, part):
    key = jax.random.fold_in(key, 31)
    return blended(key, (EXPERTS, D, H), (1, D, H), D)


def draw_w_down(key, part):
    key = jax.random.fold_in(key, 37)
    return blended(key, (D, EXPERTS, H), (D, 1, H), H)


def shard_levels(key, dims, cuts, low, largest):
    factor_of = 1.0
    for position, parts in cuts:
        steps = jax.random.uniform(jax.random.fold_in(jax.random.fold_in(key, 6), position), (parts,), jnp.float32, low / len(cuts), largest / len(cuts))
        factor_of = factor_of * jnp.repeat(jnp.exp(steps), dims[position] // parts).reshape((-1,) + (1,) * (len(dims) - 1 - position))
    return factor_of


def assign_block(stream_key, own, number, rows, count, top, most, skew):
    ranking = jax.random.permutation(stream_key, count)
    packed, usual = shares(count, rows * top, most, skew, True), shares(count, rows * top, most, skew, False)
    places = jnp.arange(count)

    def named(lengths, offset_by):
        used = int((lengths > 0).sum())
        fixed = max(1, used // 4)
        passed = fixed + (places - fixed + offset_by * (used - fixed)) % max(1, count - fixed)
        return jnp.zeros((count,), jnp.int32).at[ranking[jnp.where(places < fixed, places, passed)]].set(jnp.asarray(lengths, jnp.int32))

    lengths = jnp.where(number % 4 == 0, named(packed, number // 4), named(usual, number - number // 4 - 1))
    mixed = jax.random.permutation(jax.random.fold_in(own, 3), count)
    donor, taker = mixed[0:count // 2 * 2:2], mixed[1:count // 2 * 2:2]
    room = jnp.minimum(lengths[donor] - 1, most - lengths[taker]) // 2
    room = jnp.where((donor == ranking[0]) | (taker == ranking[0]) | (lengths[taker] == 0), 0, jnp.maximum(room, 0))
    passed = jax.random.randint(jax.random.fold_in(own, 4), (count // 2,), 0, 1 << 20) % (room + 1)
    lengths = lengths.at[donor].add(-passed).at[taker].add(passed)
    members = jnp.searchsorted(jnp.cumsum(lengths), jnp.arange(rows * top), side="right").astype(jnp.int32)
    grid = members.reshape(top, rows).T
    grid = grid[jax.random.permutation(jax.random.fold_in(own, 1), rows)]
    offset_by = jax.random.randint(jax.random.fold_in(own, 2), (rows, 1), 0, top)
    return jnp.take_along_axis(grid, (jnp.arange(top)[None, :] + offset_by) % top, axis=1)


def shares(amount, total, most, skew, full):
    loads = [(1 << 20) // math.isqrt(grade ** skew) + 1 for grade in range(1, amount + 1)]
    largest = most if full else min(most, max(-(-total // amount), total * loads[0] // sum(loads)))
    least = 1 if total - largest >= amount - 1 else 0
    counts, rest = [largest] + [least] * (amount - 1), total - largest - least * (amount - 1)
    while rest > 0:
        free = [i for i in range(1, amount) if counts[i] < largest] or [i for i in range(1, amount) if counts[i] < most]
        mass, left = sum([loads[i] for i in free]), rest
        for i in free:
            more = min(most - counts[i], max(1, left * loads[i] // mass), rest)
            counts[i] = counts[i] + more
            rest = rest - more
    return np.array(counts)


def setup_inputs(seed: int = 0) -> dict:
    splits = jax.random.split(jax.random.key(seed), 10)
    tokens = draw_tokens(jax.random.fold_in(splits[9], 71), 0)
    targets = draw_targets(jax.random.fold_in(splits[9], 71), 0)
    routes_keys = jax.random.split(jax.random.fold_in(splits[2], 1), TOKENS // TOK_DEV)
    routes_turns = jax.random.permutation(jax.random.fold_in(splits[2], 3), TOKENS // TOK_DEV)
    routes = jax.vmap(lambda own, number: assign_block(jax.random.fold_in(splits[2], 2), own, number, TOK_DEV, EXPERTS, TOP, CAP, 0))(routes_keys, routes_turns).reshape((TOKENS, TOP))
    route_logits = jnp.clip(jax.random.uniform(splits[3], (TOKENS, TOP), jnp.float32, -3.0, 3.0) * shard_levels(splits[3], (TOKENS, TOP), ((0, 512),), -0.4, 0.0), -3.0, 3.0)
    slot_order = jax.vmap(lambda own: jax.random.permutation(own, TOP))(jax.random.split(splits[4], TOKENS)).reshape((TOKENS, TOP)).astype(jnp.int32)
    seq_ids = draw_seq_ids(jax.random.fold_in(splits[9], 71), 0)
    w_gate = draw_w_gate(jax.random.fold_in(splits[9], 71), 0)
    w_up = draw_w_up(jax.random.fold_in(splits[9], 71), 0)
    w_down = draw_w_down(jax.random.fold_in(splits[9], 71), 0)
    return {"tokens": tokens, "targets": targets, "routes": routes, "route_logits": route_logits, "slot_order": slot_order, "seq_ids": seq_ids, "w_gate": w_gate, "w_up": w_up, "w_down": w_down}


radius_factor = 2.0

def unchanged(single_value):
    return single_value

def dual_search(seq_loss, pair_total, one_total):
    sum_total = one_total(jnp.sum(seq_loss))

    def advance(step_index, bounds):
        lower, upper = bounds
        middle = 0.5 * (lower + upper)
        excess = jnp.maximum(seq_loss - middle, 0.0)
        square_sum, plain_sum = pair_total((jnp.sum(excess * excess), jnp.sum(excess)))
        is_above = NSEQ * square_sum - radius_factor * plain_sum * plain_sum >= 0.0
        return (jnp.where(is_above, lower, middle), jnp.where(is_above, middle, upper))
    lower, upper = lax.fori_loop(0, BISECT_STEPS, advance, (-sum_total, sum_total))
    excess = jnp.maximum(seq_loss - 0.5 * (lower + upper), 0.0)
    return excess / one_total(jnp.sum(excess))

def route_gates(route_logits, slot_order):
    picked = jnp.take_along_axis(route_logits, slot_order, axis=1)
    raised = jnp.exp(picked)
    return raised / lax.optimization_barrier(jnp.sum(raised, axis=1, keepdims=True))

def reference(tokens, targets, routes, route_logits, slot_order, seq_ids, w_gate, w_up, w_down):
    slot_count = TOKENS * TOP
    per_expert = slot_count // EXPERTS
    gate_probs = route_gates(route_logits, slot_order)
    flat_route = routes.reshape(slot_count)
    slot_sorted = jnp.argsort(flat_route, stable=True).astype(jnp.int32)
    grouped = slot_sorted.reshape(EXPERTS, per_expert)
    flat_gates = gate_probs.reshape(slot_count)

    def expert_forward(combined, expert):
        chosen = grouped[expert]
        token_rows = tokens[chosen // TOP]
        gate_proj = jnp.dot(token_rows, w_gate[expert], preferred_element_type=jnp.float32)
        up_proj = jnp.dot(token_rows, w_up[expert], preferred_element_type=jnp.float32)
        hidden = (jax.nn.silu(gate_proj) * up_proj).astype(jnp.bfloat16)
        down_slice = lax.dynamic_index_in_dim(w_down, expert, 1, keepdims=False)
        expert_out = jnp.dot(hidden, down_slice.T, preferred_element_type=jnp.float32).astype(jnp.bfloat16)
        weighted = flat_gates[chosen][:, None] * expert_out.astype(jnp.float32)
        combined = combined.at[chosen // TOP].add(weighted)
        return (combined, hidden)
    combined, hidden_all = lax.scan(expert_forward, jnp.zeros((TOKENS, D), jnp.float32), jnp.arange(EXPERTS, dtype=jnp.int32))
    error = combined - targets.astype(jnp.float32)
    seq_sq = jax.ops.segment_sum(lax.optimization_barrier(jnp.sum(error * error, axis=1)), seq_ids, num_segments=NSEQ)
    seq_len = jax.ops.segment_sum(jnp.ones((TOKENS,), jnp.float32), seq_ids, num_segments=NSEQ)
    seq_loss = seq_sq / (seq_len * D)
    dual_weight = dual_search(seq_loss, unchanged, unchanged)
    seq_rate = dual_weight / seq_len
    slot_weight = GRAD_SCALE * gate_probs * seq_rate[seq_ids][:, None]
    flat_weight = slot_weight.reshape(slot_count)
    error_low = error.astype(jnp.bfloat16)

    def expert_grad(expert):
        chosen = grouped[expert]
        scaled = (flat_weight[chosen][:, None] * hidden_all[expert].astype(jnp.float32)).astype(jnp.bfloat16)
        return jnp.dot(error_low[chosen // TOP].T, scaled, preferred_element_type=jnp.float32)
    grad_stack = lax.map(expert_grad, jnp.arange(EXPERTS, dtype=jnp.int32))
    return (combined.astype(jnp.bfloat16), seq_loss, dual_weight, jnp.transpose(grad_stack, (1, 0, 2)))
```

```python
import functools

import jax
import jax.numpy as jnp
from jax import lax
from jax.experimental import pallas as pl
from jax.experimental.pallas import tpu as pltpu
from jax.sharding import PartitionSpec as P

MESH = pl.DeviceIdType.MESH
SIDE = 4
NSEQ = 64
CAP = 64
EXPERTS = 16
ROWS_INFO = 40
F32 = jnp.float32
BF16 = jnp.bfloat16


def position():
    dp, expert = lax.axis_index("dp"), lax.axis_index("expert")
    return dp // 2, dp % 2, expert // SIDE, expert % SIDE


def place(z, core, x, y, dz=0, dx=0, dy=0, nz=1, other=False):
    zz = lax.rem(z + dz + nz, nz) if dz else z
    cc = 1 - core if other else core
    xx = lax.rem(x + dx + SIDE, SIDE)
    yy = lax.rem(y + dy + SIDE, SIDE)
    return {"dp": zz * 2 + cc, "expert": xx * SIDE + yy}


def remote(src, dst, send, recv, device):
    return pltpu.make_async_remote_copy(
        src_ref=src, dst_ref=dst, send_sem=send, recv_sem=recv, device_id=device, device_id_type=MESH
    )


def meet(devices):
    barrier = pltpu.get_barrier_semaphore()
    for device in devices:
        pl.semaphore_signal(barrier, inc=1, device_id=device, device_id_type=MESH)
    pl.semaphore_wait(barrier, len(devices))


def hot_rows(rank_row):
    rows = lax.broadcasted_iota(jnp.int32, (CAP, rank_row.shape[1]), 0).astype(F32)
    return rank_row == rows


def rank_row(infos, f, d, x, y, ef, ed):
    expert = lax.rem(x + ed, SIDE) * SIDE + lax.rem(y + ef, SIDE)
    return infos[f, d, pl.ds(expert, 1), :]


def selection(infos, half, step, x, y):
    parts = []
    for other in range(SIDE):
        if half == 0:
            row = rank_row(infos, 0, step, x, y, other, 0)
        else:
            row = rank_row(infos, step, 0, x, y, 0, other)
        parts.append(hot_rows(row))
    return jnp.where(jnp.concatenate(parts, axis=0), 1.0, 0.0).astype(BF16)


class Dispatch:
    def __init__(self, source, wide, sent, rows, s1, r1, s2, r2, here):
        self.source, self.wide, self.sent, self.rows = source, wide, sent, rows
        self.s1, self.r1, self.s2, self.r2 = s1, r1, s2, r2
        self.here = here
        self.width = source.shape[1] // 2

    def peer(self, half, step):
        return place(*self.here, dx=step) if half == 0 else place(*self.here, dy=step)

    def first(self, half, step):
        src = self.source.at[:, pl.ds(half * self.width, self.width)]
        return remote(
            src, self.wide.at[half, step - 1], self.s1.at[half, step - 1], self.r1.at[half, step - 1],
            self.peer(half, step),
        )

    def second(self, half, f, d):
        hop = f if half == 0 else d
        return remote(
            self.sent.at[half, f, d], self.rows.at[half, f, d], self.s2.at[half, f, d], self.r2.at[half, f, d],
            self.peer(1 - half, hop),
        )

    def start(self):
        for step in (2, 1, 3):
            for half in range(2):
                self.first(half, step).start()

    def forward(self, infos, half, step):
        _, _, x, y = self.here
        if step:
            self.first(half, step).wait_recv()
            block = self.wide[half, step - 1]
        else:
            block = self.source[:, half * self.width : (half + 1) * self.width]
        picked = jnp.dot(selection(infos, half, step, x, y), block, preferred_element_type=F32)
        for hop in (2, 1, 3, 0):
            f, d = (hop, step) if half == 0 else (step, hop)
            value = picked[hop * CAP : (hop + 1) * CAP].astype(BF16)
            if hop:
                self.sent[half, f, d] = value
                self.second(half, f, d).start()
            else:
                self.rows[half, f, d] = value

    def arrived(self, f):
        for d in range(SIDE):
            if f:
                self.second(0, f, d).wait_recv()
            if d:
                self.second(1, f, d).wait_recv()

    def finish(self):
        for half in range(2):
            for step in range(1, SIDE):
                self.first(half, step).wait_send()
            for a in range(SIDE):
                for hop in range(1, SIDE):
                    f, d = (hop, a) if half == 0 else (a, hop)
                    self.second(half, f, d).wait_send()


def forward_kernel(
    nz, tokens, targets, info, seq_column, w_gate, w_up, w_down,
    mixed, error_low, hidden, infos, partial,
    down, wide, sent, rows, outs, back, part_out, part_in,
    i_s, i_r, s1, r1, s2, r2, w_s, w_r, b_s, b_r, p_s, p_r,
):
    here = position()
    z, core, x, y = here
    width = tokens.shape[1] // 2
    ring = lambda dz: place(*here, dz=dz, nz=nz)
    peers = [place(*here, dx=step) for step in range(1, SIDE)] + [place(*here, dy=step) for step in range(1, SIDE)]
    peers.append(place(*here, other=True, nz=nz))
    if nz > 1:
        peers += [ring(1), ring(-1)]
    meet(peers)

    infos[0, 0] = info[...]

    def info_x(step):
        return remote(info, infos.at[0, step], i_s.at[0, step - 1], i_r.at[0, step - 1], place(*here, dx=step))

    def info_y(step):
        return remote(infos.at[0], infos.at[step], i_s.at[1, step - 1], i_r.at[1, step - 1], place(*here, dy=step))

    for step in range(1, SIDE):
        info_x(step).start()
    go = Dispatch(tokens, wide, sent, rows, s1, r1, s2, r2, here)
    go.start()

    ups, downs = nz // 2, nz - 1 - nz // 2

    def gather(way, step):
        block = lax.rem(z - step + nz, nz) if way == 0 else lax.rem(z + step, nz)
        ref = down.at[block, core]
        src = w_down if step == 0 else ref
        return remote(src, ref, w_s.at[way, step], w_r.at[way, step], ring(1 if way == 0 else -1))

    down[z, core] = w_down[...]

    def gather_step(step):
        for way, count in ((0, ups), (1, downs)):
            if 0 < step <= count:
                gather(way, step - 1).wait_recv()
            if step < count:
                gather(way, step).start()

    gather_step(0)
    for step in range(1, SIDE):
        info_x(step).wait_recv()
    for step in range(1, SIDE):
        info_y(step).start()
    go.forward(infos, 0, 0)
    gather_step(1)
    for step in range(1, SIDE):
        info_y(step).wait_recv()
    go.forward(infos, 1, 0)
    gather_step(2)
    tick = 3
    for step in (1, 3, 2):
        for half in range(2):
            go.forward(infos, half, step)
            gather_step(tick)
            tick += 1
    for step in range(tick, max(ups, downs) + 1):
        gather_step(step)
    twin = remote(down.at[:, core], down.at[:, core], w_s.at[0, ups], w_r.at[0, ups], place(*here, other=True, nz=nz))
    twin.start()
    twin.wait_send()
    twin_in = remote(
        down.at[:, 1 - core], down.at[:, 1 - core], w_s.at[0, ups], w_r.at[0, ups], place(*here, other=True, nz=nz)
    )
    twin_in.wait_recv()

    def home(half, f, d):
        if half == 0:
            return remote(
                outs.at[0, f], back.at[0, f], b_s.at[0, f, 0], b_r.at[0, f, 0], place(*here, dy=-f)
            )
        return remote(outs.at[1, f, d], back.at[1, f, d], b_s.at[1, f, d], b_r.at[1, f, d], place(*here, dx=-d))

    for f in range(SIDE):
        go.arrived(f)
        gate = jnp.zeros((SIDE * CAP, w_gate.shape[1]), F32)
        up = jnp.zeros((SIDE * CAP, w_gate.shape[1]), F32)
        for half in range(2):
            block = rows[half, f].reshape(SIDE * CAP, width)
            gate = gate + jnp.dot(block, w_gate[half * width : (half + 1) * width], preferred_element_type=F32)
            up = up + jnp.dot(block, w_up[half * width : (half + 1) * width], preferred_element_type=F32)
        unit = ((gate / (1.0 + jnp.exp(-gate))) * up).astype(BF16)
        hidden[f] = unit
        weights = []
        for d in range(SIDE):
            own = x * SIDE + y
            ranks, gates = infos[f, d, pl.ds(own, 1), :], infos[f, d, pl.ds(own + EXPERTS, 1), :]
            weights.append(jnp.sum(jnp.where(hot_rows(ranks), gates, 0.0), axis=1, keepdims=True))
        weight = jnp.concatenate(weights, axis=0)
        for half in range(2):
            matrix = down[half * nz // 2 : (half + 1) * nz // 2].reshape(width, -1)
            value = lax.dot_general(unit, matrix, (((1,), (1,)), ((), ())), preferred_element_type=F32)
            value = (value * weight).astype(BF16).reshape(SIDE, CAP, width)
            if half == 0:
                if f:
                    outs[0, f] = value
                    home(0, f, 0).start()
                else:
                    back[0, 0] = value
            else:
                for d in range(SIDE):
                    if d:
                        outs[1, f, d] = value[d]
                        home(1, f, d).start()
                    else:
                        back[1, f, 0] = value[0]

    def share(half, step):
        device = place(*here, dx=-step) if half == 0 else place(*here, dy=-step)
        return remote(
            part_out.at[half, step - 1], part_in.at[half, step - 1], p_s.at[half, step - 1], p_r.at[half, step - 1], device
        )

    own_parts = []
    for half in range(2):
        if half == 0:
            for f in range(1, SIDE):
                home(0, f, 0).wait_recv()
        for step in (2, 1, 3, 0):
            if half == 0:
                block = back[0, :, step].reshape(SIDE * CAP, width)
            else:
                for d in range(1, SIDE):
                    home(1, step, d).wait_recv()
                block = back[1, step].reshape(SIDE * CAP, width)
            total = lax.dot_general(
                selection(infos, half, step, x, y), block, (((0,), (0,)), ((), ())), preferred_element_type=F32
            )
            if step:
                part_out[half, step - 1] = total.astype(BF16)
                share(half, step).start()
            else:
                own_parts.append(total)
    squares = jnp.zeros((tokens.shape[0], 1), F32)
    for half in range(2):
        total = own_parts[half]
        for step in range(1, SIDE):
            share(half, step).wait_recv()
            total = total + part_in[half, step - 1].astype(F32)
        columns = slice(half * width, (half + 1) * width)
        mixed[:, columns] = total.astype(BF16)
        error = total - targets[:, columns].astype(F32)
        error_low[:, columns] = error.astype(BF16)
        squares = squares + jnp.sum(error * error, axis=1, keepdims=True)
    lane = lax.broadcasted_iota(jnp.int32, (tokens.shape[0], 2 * NSEQ), 1)
    number = jnp.where(lane < NSEQ, lane, lane - NSEQ)
    entry = jnp.where(lane < NSEQ, squares, 1.0)
    sums = jnp.sum(jnp.where(seq_column[...] == number, entry, 0.0), axis=0, keepdims=True)
    partial[...] = jnp.broadcast_to(sums, partial.shape)

    go.finish()
    for step in range(1, SIDE):
        info_x(step).wait_send()
        info_y(step).wait_send()
        share(0, step).wait_send()
        share(1, step).wait_send()
        home(0, step, 0).wait_send()
        for f in range(SIDE):
            home(1, f, step).wait_send()
    for way, count in ((0, ups), (1, downs)):
        for step in range(count):
            gather(way, step).wait_send()


def dual_search(loss_column):
    lane = lax.broadcasted_iota(jnp.int32, (1, 128), 1).astype(F32)
    upper = jnp.sum(loss_column, axis=0, keepdims=True)
    lower = -upper
    for bits in (7, 7, 7, 7, 7, 5):
        ways = float(2**bits)
        width = (upper - lower) / ways
        middle = lower + width * (lane + 1.0)
        excess = jnp.maximum(loss_column - middle, 0.0)
        plain = jnp.sum(excess, axis=0, keepdims=True)
        square = jnp.sum(excess * excess, axis=0, keepdims=True)
        below = (NSEQ * square - 2.0 * plain * plain < 0.0) & (lane < ways - 1.0)
        count = jnp.sum(jnp.where(below, 1.0, 0.0), axis=1, keepdims=True)
        lower, upper = lower + width * count, lower + width * (count + 1.0)
    return 0.5 * (lower + upper)


def backward_kernel(
    nz, scale, features, error, hidden, infos, partial,
    grad, losses,
    wide, sent, rows, total, seen, grads, twin_in, ring_out, ring_in,
    s1, r1, s2, r2, a_s, a_r, t_s, t_r, g_s, g_r,
):
    here = position()
    z, core, x, y = here
    width = error.shape[1] // 2
    ring = lambda dz: place(*here, dz=dz, nz=nz)
    peers = [place(*here, dx=step) for step in range(1, SIDE)] + [place(*here, dy=step) for step in range(1, SIDE)]
    peers.append(place(*here, other=True, nz=nz))
    strides = []
    stride = 1
    while stride < nz:
        strides.append(stride)
        stride *= 2

    def across(stride):
        bit = lax.rem(z // stride, 2)
        return {"dp": (z + stride - 2 * stride * bit) * 2 + core, "expert": x * SIDE + y}

    for stride in strides:
        peers.append(across(stride))
    if nz > 1:
        peers += [ring(1), ring(-1)]
    meet(peers)

    go = Dispatch(error, wide, sent, rows, s1, r1, s2, r2, here)
    go.start()

    stages = [
        [place(*here, dx=step) for step in range(1, SIDE)],
        [place(*here, dy=step) for step in range(1, SIDE)],
        [place(*here, other=True, nz=nz)],
    ] + [[across(stride)] for stride in strides]
    total[0] = partial[...]

    def tell(stage, index):
        return remote(
            total.at[stage], seen.at[stage, index], a_s.at[stage, index], a_r.at[stage, index], stages[stage][index]
        )

    def stage_start(stage):
        for index in range(len(stages[stage])):
            tell(stage, index).start()

    def stage_end(stage):
        value = total[stage]
        for index in range(len(stages[stage])):
            tell(stage, index).wait_recv()
            value = value + seen[stage, index]
        total[stage + 1] = value
        if stage + 1 < len(stages):
            stage_start(stage + 1)

    stage_start(0)
    done = 0
    for step in (0, 1, 3, 2):
        for half in range(2):
            go.forward(infos, half, step)
            if done < len(stages):
                stage_end(done)
                done += 1
    while done < len(stages):
        stage_end(done)
        done += 1

    sums = total[len(stages)][0:1]
    lengths = pltpu.roll(sums, NSEQ, 1)
    loss_row = sums / (lengths * float(features))
    eye = lax.broadcasted_iota(jnp.int32, (NSEQ, 128), 0) == lax.broadcasted_iota(jnp.int32, (NSEQ, 128), 1)
    column = lambda row: jnp.sum(jnp.where(eye, row, 0.0), axis=1, keepdims=True)
    loss_column = column(loss_row)
    eta = dual_search(loss_column)
    excess_column = jnp.maximum(loss_column - eta, 0.0)
    norm = jnp.sum(excess_column, axis=0, keepdims=True)
    dual_row = jnp.maximum(loss_row - eta, 0.0) / norm
    losses[0:1, :] = loss_row
    losses[1:2, :] = dual_row
    rate = (excess_column / norm) / column(lengths)

    own = x * SIDE + y
    numbers = lax.broadcasted_iota(jnp.int32, (NSEQ, 128), 0).astype(F32)
    scaled = []
    for f in range(SIDE):
        weights = []
        for d in range(SIDE):
            ranks, gates = infos[f, d, pl.ds(own, 1), :], infos[f, d, pl.ds(own + EXPERTS, 1), :]
            seq_row = infos[f, d, 2 * EXPERTS : 2 * EXPERTS + 1, :]
            token_rate = jnp.sum(jnp.where(seq_row == numbers, rate, 0.0), axis=0, keepdims=True)
            token_weight = (scale * gates) * token_rate
            weights.append(jnp.sum(jnp.where(hot_rows(ranks), token_weight, 0.0), axis=1, keepdims=True))
        weight = jnp.concatenate(weights, axis=0)
        scaled.append((hidden[f].astype(F32) * weight).astype(BF16))
    scaled = jnp.concatenate(scaled, axis=0)

    for f in range(SIDE):
        go.arrived(f)
    block = 64
    chunk = 4 * block * 2
    for half in range(2):
        for part in range(width // chunk):
            value = lax.dot_general(
                rows[half, :, :, :, part * chunk : (part + 1) * chunk].reshape(SIDE * SIDE * CAP, chunk),
                scaled, (((0,), (0,)), ((), ())), preferred_element_type=F32,
            )
            first = (half * width + part * chunk) // (2 * block)
            grads[first : first + chunk // (2 * block)] = value.reshape(chunk // (2 * block), 2, block, -1)

    twin = remote(grads.at[:, 1 - core], twin_in, t_s, t_r, place(*here, other=True, nz=nz))
    twin.start()
    twin.wait_recv()

    def own_part(target):
        return grads[target, core] + twin_in[target]

    ups, downs = nz // 2 - 1, nz // 2

    def pass_on(way, step):
        return remote(
            ring_out.at[way, step], ring_in.at[way, step], g_s.at[way, step], g_r.at[way, step],
            ring(1 if way == 0 else -1),
        )

    for step in range(downs):
        for way, count in ((0, ups), (1, downs)):
            if step < count:
                target = lax.rem(z + count - step, nz) if way == 0 else lax.rem(z - count + step + nz, nz)
                value = own_part(target)
                if step:
                    pass_on(way, step - 1).wait_recv()
                    value = value + ring_in[way, step - 1]
                ring_out[way, step] = value
                pass_on(way, step).start()
    value = own_part(z)
    for way, count in ((0, ups), (1, downs)):
        if count:
            pass_on(way, count - 1).wait_recv()
            value = value + ring_in[way, count - 1]
    grad[...] = value

    go.finish()
    twin.wait_send()
    for way, count in ((0, ups), (1, downs)):
        for step in range(count):
            pass_on(way, step).wait_send()
    for stage in range(len(stages)):
        for index in range(len(stages[stage])):
            tell(stage, index).wait_send()


def local(nz, tokens, targets, routes, route_logits, slot_order, seq_ids, w_gate, w_up, w_down):
    tok, feat = tokens.shape
    top = routes.shape[1]
    units = w_gate.shape[2]
    scale = float(tok * lax.axis_size("dp") * lax.axis_size("expert") // 8)
    width = feat // 2

    routes_t, logits_t, order_t = routes.T, route_logits.T, slot_order.T
    slots = lax.broadcasted_iota(jnp.int32, (1, top, 1), 1)
    picked = jnp.sum(jnp.where(order_t[:, None, :] == slots, logits_t[None, :, :], 0.0), axis=1)
    raised = jnp.exp(picked)
    gates = raised / jnp.sum(raised, axis=0, keepdims=True)
    hot = routes_t[None, :, :] == lax.broadcasted_iota(jnp.int32, (EXPERTS, 1, 1), 0)
    named = jnp.sum(jnp.where(hot, 1.0, 0.0), axis=1)
    gate_of = jnp.sum(jnp.where(hot, gates[None], 0.0), axis=1)
    earlier = lax.broadcasted_iota(jnp.int32, (tok, tok), 0) < lax.broadcasted_iota(jnp.int32, (tok, tok), 1)
    ranks = jnp.dot(named.astype(BF16), earlier.astype(BF16), preferred_element_type=F32)
    ranks = jnp.where(named > 0.5, ranks, -1.0)
    seq_rows = jnp.broadcast_to(seq_ids.astype(F32)[None, :], (ROWS_INFO - 2 * EXPERTS, tok))
    info = jnp.concatenate([ranks, gate_of, seq_rows], axis=0)

    vmem = pl.BlockSpec(memory_space=pltpu.VMEM)
    dma = pltpu.SemaphoreType.DMA
    travel = [
        pltpu.VMEM((2, SIDE - 1, tok, width), BF16),
        pltpu.VMEM((2, SIDE, SIDE, CAP, width), BF16),
        pltpu.VMEM((2, SIDE, SIDE, CAP, width), BF16),
    ]
    travel_sems = [
        dma((2, SIDE - 1)), dma((2, SIDE - 1)), dma((2, SIDE, SIDE)), dma((2, SIDE, SIDE)),
    ]
    flops = 2 * EXPERTS * CAP * feat * units
    mixed, error_low, hidden, infos, partial = pl.pallas_call(
        functools.partial(forward_kernel, nz),
        out_shape=(
            jax.ShapeDtypeStruct((tok, feat), BF16),
            jax.ShapeDtypeStruct((tok, feat), BF16),
            jax.ShapeDtypeStruct((SIDE, SIDE * CAP, units), BF16),
            jax.ShapeDtypeStruct((SIDE, SIDE, ROWS_INFO, tok), F32),
            jax.ShapeDtypeStruct((8, 128), F32),
        ),
        in_specs=[vmem] * 7,
        out_specs=[vmem] * 5,
        scratch_shapes=[
            pltpu.VMEM((nz, 2, feat // (2 * nz), units), BF16),
            *travel,
            pltpu.VMEM((2, SIDE, SIDE, CAP, width), BF16),
            pltpu.VMEM((2, SIDE, SIDE, CAP, width), BF16),
            pltpu.VMEM((2, SIDE - 1, tok, width), BF16),
            pltpu.VMEM((2, SIDE - 1, tok, width), BF16),
            dma((2, SIDE - 1)), dma((2, SIDE - 1)),
            *travel_sems,
            dma((2, nz // 2 + 1)), dma((2, nz // 2 + 1)),
            dma((2, SIDE, SIDE)), dma((2, SIDE, SIDE)),
            dma((2, SIDE - 1)), dma((2, SIDE - 1)),
        ],
        compiler_params=pltpu.CompilerParams(
            collective_id=0, has_side_effects=True, vmem_limit_bytes=56 * 2**20
        ),
        cost_estimate=pl.CostEstimate(flops=3 * flops, bytes_accessed=8 * 2**20, transcendentals=0),
        name="forward",
    )(tokens, targets, info, seq_ids[:, None], w_gate[0], w_up[0], w_down[:, 0])

    block = feat // (2 * nz)
    stages = 3 + (nz - 1).bit_length()
    grad, losses = pl.pallas_call(
        functools.partial(backward_kernel, nz, scale, feat),
        out_shape=(
            jax.ShapeDtypeStruct((block, units), F32),
            jax.ShapeDtypeStruct((8, 128), F32),
        ),
        in_specs=[vmem] * 4,
        out_specs=[vmem] * 2,
        scratch_shapes=[
            *travel,
            pltpu.VMEM((stages + 1, 8, 128), F32),
            pltpu.VMEM((stages, SIDE - 1, 8, 128), F32),
            pltpu.VMEM((nz, 2, block, units), F32),
            pltpu.VMEM((nz, block, units), F32),
            pltpu.VMEM((2, nz // 2, block, units), F32),
            pltpu.VMEM((2, nz // 2, block, units), F32),
            *travel_sems,
            dma((stages, SIDE - 1)), dma((stages, SIDE - 1)),
            dma, dma,
            dma((2, nz // 2)), dma((2, nz // 2)),
        ],
        compiler_params=pltpu.CompilerParams(
            collective_id=1, has_side_effects=True, vmem_limit_bytes=56 * 2**20
        ),
        cost_estimate=pl.CostEstimate(flops=flops, bytes_accessed=8 * 2**20, transcendentals=0),
        name="backward",
    )(error_low, hidden, infos, partial)
    return (mixed, losses[0, :NSEQ], losses[1, :NSEQ], grad[:, None, :])


def solution(mesh):
    return jax.shard_map(
        functools.partial(local, mesh.shape["dp"] // 2),
        mesh=mesh,
        in_specs=(
            P(("dp", "expert"), None),
            P(("dp", "expert"), None),
            P(("dp", "expert"), None),
            P(("dp", "expert"), None),
            P(("dp", "expert"), None),
            P(("dp", "expert")),
            P("expert", None, None),
            P("expert", None, None),
            P("dp", "expert", None),
        ),
        out_specs=(P(("dp", "expert"), None), P(), P(), P("dp", "expert", None)),
        check_vma=False,
    )
```

```python
import functools

import jax
import jax.numpy as jnp
from jax import lax
from jax.experimental import pallas as pl
from jax.experimental.pallas import tpu as pltpu
from jax.sharding import PartitionSpec as P

MESH = pl.DeviceIdType.MESH
SIDE = 4
NSEQ = 64
CAP = 64
EXPERTS = 16
ROWS_INFO = 40
PASSES = 4
CUTS = 4
LANES = 128
F32 = jnp.float32
BF16 = jnp.bfloat16


def position():
    dp, expert = lax.axis_index("dp"), lax.axis_index("expert")
    return dp // 2, dp % 2, expert // SIDE, expert % SIDE


def place(z, core, x, y, dz=0, dx=0, dy=0, nz=1, other=False):
    zz = lax.rem(z + dz + nz, nz) if dz else z
    cc = 1 - core if other else core
    xx = lax.rem(x + dx + SIDE, SIDE)
    yy = lax.rem(y + dy + SIDE, SIDE)
    return {"dp": zz * 2 + cc, "expert": xx * SIDE + yy}


def remote(src, dst, send, recv, device):
    return pltpu.make_async_remote_copy(
        src_ref=src, dst_ref=dst, send_sem=send, recv_sem=recv, device_id=device, device_id_type=MESH
    )


def meet(devices):
    barrier = pltpu.get_barrier_semaphore()
    for device in devices:
        pl.semaphore_signal(barrier, inc=1, device_id=device, device_id_type=MESH)
    pl.semaphore_wait(barrier, len(devices))


def hot_rows(rank_row):
    rows = lax.broadcasted_iota(jnp.int32, (CAP, rank_row.shape[1]), 0).astype(F32)
    return rank_row == rows


def rank_row(infos, f, d, x, y, ef, ed):
    expert = lax.rem(x + ed, SIDE) * SIDE + lax.rem(y + ef, SIDE)
    return infos[f, d, pl.ds(expert, 1), :]


def selection(infos, half, step, x, y):
    parts = []
    for other in range(SIDE):
        if half == 0:
            row = rank_row(infos, 0, step, x, y, other, 0)
        else:
            row = rank_row(infos, step, 0, x, y, 0, other)
        parts.append(hot_rows(row))
    return jnp.where(jnp.concatenate(parts, axis=0), 1.0, 0.0).astype(BF16)


class Dispatch:
    def __init__(self, source, wide, sent, rows, s1, r1, s2, r2, here):
        self.source, self.wide, self.sent, self.rows = source, wide, sent, rows
        self.s1, self.r1, self.s2, self.r2 = s1, r1, s2, r2
        self.here = here
        self.width = source.shape[1] // 2

    def peer(self, half, step):
        return place(*self.here, dx=step) if half == 0 else place(*self.here, dy=step)

    def first(self, half, step):
        src = self.source.at[:, pl.ds(half * self.width, self.width)]
        return remote(
            src, self.wide.at[half, step - 1], self.s1.at[half, step - 1], self.r1.at[half, step - 1],
            self.peer(half, step),
        )

    def second(self, half, f, d):
        hop = f if half == 0 else d
        return remote(
            self.sent.at[half, f, d], self.rows.at[half, f, d], self.s2.at[half, f, d], self.r2.at[half, f, d],
            self.peer(1 - half, hop),
        )

    def start(self):
        for step in (2, 1, 3):
            for half in range(2):
                self.first(half, step).start()

    def forward(self, infos, half, step, send=True):
        _, _, x, y = self.here
        if step:
            self.first(half, step).wait_recv()
            block = self.wide[half, step - 1]
        else:
            block = self.source[:, half * self.width : (half + 1) * self.width]
        picked = jnp.dot(selection(infos, half, step, x, y), block, preferred_element_type=F32)
        for hop in (2, 1, 3, 0):
            f, d = (hop, step) if half == 0 else (step, hop)
            value = picked[hop * CAP : (hop + 1) * CAP].astype(BF16)
            if hop:
                self.sent[half, f, d] = value
                if send:
                    self.second(half, f, d).start()
            else:
                self.rows[half, f, d] = value

    def arrived(self, f):
        for d in range(SIDE):
            if f:
                self.second(0, f, d).wait_recv()
            if d:
                self.second(1, f, d).wait_recv()

    def finish(self):
        for half in range(2):
            for step in range(1, SIDE):
                self.first(half, step).wait_send()
            for a in range(SIDE):
                for hop in range(1, SIDE):
                    f, d = (hop, a) if half == 0 else (a, hop)
                    self.second(half, f, d).wait_send()


def dual_search(loss_column):
    lane = lax.broadcasted_iota(jnp.int32, (1, 128), 1).astype(F32)
    upper = jnp.sum(loss_column, axis=0, keepdims=True)
    lower = -upper
    for bits in (7, 7, 7, 7, 7, 5):
        ways = float(2**bits)
        width = (upper - lower) / ways
        middle = lower + width * (lane + 1.0)
        excess = jnp.maximum(loss_column - middle, 0.0)
        plain = jnp.sum(excess, axis=0, keepdims=True)
        square = jnp.sum(excess * excess, axis=0, keepdims=True)
        below = (NSEQ * square - 2.0 * plain * plain < 0.0) & (lane < ways - 1.0)
        count = jnp.sum(jnp.where(below, 1.0, 0.0), axis=1, keepdims=True)
        lower, upper = lower + width * count, lower + width * (count + 1.0)
    return 0.5 * (lower + upper)


def sums_over(infos, f, d, own, values=None):
    ranks, gates = infos[f, d, pl.ds(own, 1), :], infos[f, d, pl.ds(own + EXPERTS, 1), :]
    entry = gates if values is None else values(f, d, gates)
    return jnp.sum(jnp.where(hot_rows(ranks), entry, 0.0), axis=1, keepdims=True)


def column_of(row, size):
    shape = (size, row.shape[1])
    eye = lax.broadcasted_iota(jnp.int32, shape, 0) == lax.broadcasted_iota(jnp.int32, shape, 1)
    return jnp.sum(jnp.where(eye, row, 0.0), axis=1, keepdims=True)


def step_kernel(
    nz, scale, tokens, targets, info, w_gate, w_up, w_down,
    mixed, grad, losses,
    infos, hidden, down, wide, sent, rows, outs, back, part_out, part_in,
    err, err_wide, err_sent, err_rows, seen, grads, twin_in, ring_out, ring_in,
    i_s, i_r, s1, r1, s2, r2, w_s, w_r, b_s, b_r, p_s, p_r,
    e1s, e1r, e2s, e2r, a_s, a_r, t_s, t_r, g_s, g_r,
):
    here = position()
    z, core, x, y = here
    tok, feat = tokens.shape
    width = feat // 2
    own = x * SIDE + y
    ring = lambda dz: place(*here, dz=dz, nz=nz)
    twin_device = place(*here, other=True)
    low, high = z % SIDE, z // SIDE
    around = lambda index, step, size: lax.rem(index + step, size)
    stage_sizes = (SIDE, 2 * SIDE, SIDE, SIDE)
    stage_index = (x, y * 2 + core, low, high)

    def stage_device(stage, step):
        if stage == 0:
            return place(*here, dx=step)
        if stage == 1:
            to = around(y * 2 + core, step, 2 * SIDE)
            return {"dp": z * 2 + to % 2, "expert": x * SIDE + to // 2}
        if stage == 2:
            return {"dp": (high * SIDE + around(low, step, SIDE)) * 2 + core, "expert": own}
        return {"dp": (around(high, step, SIDE) * SIDE + low) * 2 + core, "expert": own}

    peers = [stage_device(stage, step) for stage in range(4) for step in range(1, stage_sizes[stage])]
    peers += [ring(1), ring(-1)]
    meet(peers)

    infos[0, 0] = info[...]

    def info_x(step):
        return remote(info, infos.at[0, step], i_s.at[0, step - 1], i_r.at[0, step - 1], place(*here, dx=step))

    def info_y(step):
        return remote(infos.at[0], infos.at[step], i_s.at[1, step - 1], i_r.at[1, step - 1], place(*here, dy=step))

    for step in range(1, SIDE):
        info_x(step).start()
    go = Dispatch(tokens, wide, sent, rows, s1, r1, s2, r2, here)
    go.start()

    ups, downs = nz // 2, nz - 1 - nz // 2

    def gather(way, step):
        block = lax.rem(z - step + nz, nz) if way == 0 else lax.rem(z + step, nz)
        ref = down.at[block, core]
        src = w_down if step == 0 else ref
        return remote(src, ref, w_s.at[way, step], w_r.at[way, step], ring(1 if way == 0 else -1))

    down[z, core] = w_down[...]

    def gather_step(step):
        for way, count in ((0, ups), (1, downs)):
            if 0 < step <= count:
                gather(way, step - 1).wait_recv()
            if step < count:
                gather(way, step).start()

    gather_step(0)
    go.forward(infos, 1, 0)
    go.forward(infos, 0, 0, send=False)
    gather_step(1)
    for step in range(1, SIDE):
        info_x(step).wait_recv()
    for step in range(1, SIDE):
        info_y(step).start()
    gather_step(2)
    tick = 3
    for step in (1, 3, 2):
        go.forward(infos, 0, step, send=False)
        gather_step(tick)
        tick += 1
    for step in range(1, SIDE):
        info_y(step).wait_recv()
    for f in (1, 3, 2):
        for d in range(SIDE):
            go.second(0, f, d).start()
        go.forward(infos, 1, f)
        gather_step(tick)
        tick += 1
    for step in range(tick, max(ups, downs) + 1):
        gather_step(step)
    twin_down = [
        remote(down.at[:, side], down.at[:, side], w_s.at[0, ups], w_r.at[0, ups], twin_device) for side in (core, 1 - core)
    ]
    twin_down[0].start()

    def home(half, f, d):
        if half == 0:
            return remote(outs.at[0, f], back.at[0, f], b_s.at[0, f, 0], b_r.at[0, f, 0], place(*here, dy=-f))
        return remote(outs.at[1, f, d], back.at[1, f, d], b_s.at[1, f, d], b_r.at[1, f, d], place(*here, dx=-d))

    def expert(f):
        go.arrived(f)
        gate = jnp.zeros((SIDE * CAP, w_gate.shape[1]), F32)
        up = jnp.zeros((SIDE * CAP, w_gate.shape[1]), F32)
        for half in range(2):
            block = rows[half, f].reshape(SIDE * CAP, width)
            gate = gate + jnp.dot(block, w_gate[half * width : (half + 1) * width], preferred_element_type=F32)
            up = up + jnp.dot(block, w_up[half * width : (half + 1) * width], preferred_element_type=F32)
        unit = ((gate / (1.0 + jnp.exp(-gate))) * up).astype(BF16)
        hidden[f] = unit
        weight = jnp.concatenate([sums_over(infos, f, d, own) for d in range(SIDE)], axis=0)
        if f == 0:
            twin_down[0].wait_send()
            twin_down[1].wait_recv()
        for half in range(2):
            matrix = down[half * nz // 2 : (half + 1) * nz // 2].reshape(width, -1)
            value = lax.dot_general(unit, matrix, (((1,), (1,)), ((), ())), preferred_element_type=F32)
            value = (value * weight).astype(BF16).reshape(SIDE, CAP, width)
            if half == 0:
                if f:
                    outs[0, f] = value
                    home(0, f, 0).start()
                else:
                    back[0, 0] = value
            else:
                for d in range(SIDE):
                    if d:
                        outs[1, f, d] = value[d]
                        home(1, f, d).start()
                    else:
                        back[1, f, 0] = value[0]

    def share(half, step):
        device = place(*here, dx=-step) if half == 0 else place(*here, dy=-step)
        return remote(
            part_out.at[half, step - 1], part_in.at[half, step - 1], p_s.at[half, step - 1], p_r.at[half, step - 1], device
        )

    def merge(half, step):
        if half == 0:
            block = back[0, :, step].reshape(SIDE * CAP, width)
        else:
            for d in range(1, SIDE):
                home(1, step, d).wait_recv()
            block = back[1, step].reshape(SIDE * CAP, width)
        total = lax.dot_general(
            selection(infos, half, step, x, y), block, (((0,), (0,)), ((), ())), preferred_element_type=F32
        )
        if step:
            part_out[half, step - 1] = total.astype(BF16)
            share(half, step).start()
        return total

    expert(0)
    expert(1)
    expert(3)
    merge(1, 1)
    expert(2)
    merge(1, 3)
    for f in range(1, SIDE):
        home(0, f, 0).wait_recv()
    for step in (2, 1, 3):
        merge(0, step)
    merge(1, 2)

    blocks = feat // LANES
    squares = jnp.zeros((tok, 1), F32)
    for half in range(2):
        total = merge(half, 0)
        for step in range(1, SIDE):
            share(half, step).wait_recv()
            total = total + part_in[half, step - 1].astype(F32)
        columns = slice(half * width, (half + 1) * width)
        mixed[:, columns] = total.astype(BF16)
        error = total - targets[:, columns].astype(F32)
        low_error = error.astype(BF16)
        for block in range(width // LANES):
            target = half * (width // LANES) + block
            err[lax.rem(target - z + blocks, blocks)] = low_error[:, block * LANES : (block + 1) * LANES]
        squares = squares + jnp.sum(error * error, axis=1, keepdims=True)
    lane = lax.broadcasted_iota(jnp.int32, (tok, 2 * NSEQ), 1)
    number = jnp.where(lane < NSEQ, lane, lane - NSEQ).astype(F32)
    entry = jnp.where(lane < NSEQ, squares, 1.0)
    seq_column = column_of(info[2 * EXPERTS : 2 * EXPERTS + 1, :], tok)
    partial = jnp.sum(jnp.where(seq_column == number, entry, 0.0), axis=0, keepdims=True)

    def tell(stage, step):
        slot = seen.at[stage, stage_index[stage]]
        return remote(slot, slot, a_s.at[stage, step - 1], a_r.at[stage, step - 1], stage_device(stage, step))

    def stage_start(stage, value):
        seen[stage, stage_index[stage]] = value
        for step in range(1, stage_sizes[stage]):
            tell(stage, step).start()

    def stage_end(stage):
        for step in range(1, stage_sizes[stage]):
            tell(stage, step).wait_recv()
        value = seen[stage, 0]
        for index in range(1, stage_sizes[stage]):
            value = value + seen[stage, index]
        if stage < 3:
            stage_start(stage + 1, value)
        return value

    stage_start(0, jnp.broadcast_to(partial, (8, 2 * NSEQ)))

    per = blocks // (2 * PASSES)

    def span(half, p):
        return blocks // 2 - per * (p + 1) if half == 0 else blocks // 2 + per * p

    def err_first(p, half, step):
        device = place(*here, dx=step) if half == 0 else place(*here, dy=step)
        return remote(
            err.at[pl.ds(span(half, p), per)], err_wide.at[p, half, step - 1],
            e1s.at[p, half, step - 1], e1r.at[p, half, step - 1], device,
        )

    def err_second(p, half, f, d):
        device = place(*here, dy=f) if half == 0 else place(*here, dx=d)
        return remote(
            err_sent.at[p, half, f, d], err_rows.at[p, half, f, d], e2s.at[p, half, f, d], e2r.at[p, half, f, d], device
        )

    def err_start(p):
        for step in (2, 1, 3):
            for half in range(2):
                err_first(p, half, step).start()

    def err_forward(p, half, step):
        if step:
            err_first(p, half, step).wait_recv()
            block = jnp.concatenate([err_wide[p, half, step - 1, i] for i in range(per)], axis=1)
        else:
            block = jnp.concatenate([err[span(half, p) + i] for i in range(per)], axis=1)
        picked = jnp.dot(selection(infos, half, step, x, y), block, preferred_element_type=F32)
        for hop in (2, 1, 3, 0):
            f, d = (hop, step) if half == 0 else (step, hop)
            value = picked[hop * CAP : (hop + 1) * CAP].astype(BF16)
            if hop:
                err_sent[p, half, f, d] = value
                err_second(p, half, f, d).start()
            else:
                err_rows[p, half, f, d] = value

    def err_pass(p):
        for step in (0, 1, 3, 2):
            for half in range(2):
                err_forward(p, half, step)

    def err_arrived(p):
        for half in range(2):
            for a in range(SIDE):
                for hop in range(1, SIDE):
                    f, d = (hop, a) if half == 0 else (a, hop)
                    err_second(p, half, f, d).wait_recv()

    block_rows = LANES // 2

    def twin(p, half):
        ref = pl.ds(span(half, p), per)
        return remote(grads.at[ref, 1 - core], twin_in.at[ref], t_s.at[p, half], t_r.at[p, half], twin_device)

    def gradient(p):
        err_arrived(p)
        for half in range(2):
            value = lax.dot_general(
                err_rows[p, half].reshape(SIDE * SIDE * CAP, per * LANES), scaled,
                (((0,), (0,)), ((), ())), preferred_element_type=F32,
            )
            grads[span(half, p) : span(half, p) + per] = value.reshape(per, 2, block_rows, -1)
            twin(p, half).start()

    cut = block_rows // CUTS
    ring_counts = (blocks // 2 - 1, blocks // 2)

    def pass_on(way, step, k):
        part = pl.ds(k * cut, cut)
        return remote(
            ring_out.at[way, step, part], ring_in.at[way, step, part], g_s.at[way, step, k], g_r.at[way, step, k],
            ring(1 if way == 0 else -1),
        )

    def own_part(block, k):
        part = pl.ds(k * cut, cut)
        return grads[block, core, part] + twin_in[block, part]

    def reduce_steps(p):
        for half in range(2):
            twin(p, half).wait_recv()
        for step in range(per * p, per * (p + 1)):
            for k in range(CUTS):
                for way in range(2):
                    if step < ring_counts[way]:
                        block = blocks // 2 - 1 - step if way == 0 else blocks // 2 + step
                        value = own_part(block, k)
                        if step:
                            pass_on(way, step - 1, k).wait_recv()
                            value = value + ring_in[way, step - 1, pl.ds(k * cut, cut)]
                        ring_out[way, step, pl.ds(k * cut, cut)] = value
                        pass_on(way, step, k).start()

    err_start(0)
    for half in range(2):
        err_forward(0, half, 0)
    err_start(1)
    stage_end(0)
    for stage, step in ((1, 1), (2, 3)):
        for half in range(2):
            err_forward(0, half, step)
        stage_end(stage)
    for half in range(2):
        err_forward(0, half, 2)
    err_start(2)
    err_pass(1)
    sums = stage_end(3)[0:1]
    err_start(3)
    lengths = pltpu.roll(sums, NSEQ, 1)
    loss_row = sums / (lengths * float(feat))
    loss_column = column_of(loss_row, NSEQ)
    eta = dual_search(loss_column)
    excess_column = jnp.maximum(loss_column - eta, 0.0)
    norm = jnp.sum(excess_column, axis=0, keepdims=True)
    losses[0:1, :] = loss_row
    losses[1:2, :] = jnp.maximum(loss_row - eta, 0.0) / norm
    rate = (excess_column / norm) / column_of(lengths, NSEQ)
    numbers = lax.broadcasted_iota(jnp.int32, (NSEQ, tok), 0).astype(F32)

    def token_weights(f, d, gates):
        seq_row = infos[f, d, 2 * EXPERTS : 2 * EXPERTS + 1, :]
        return (scale * gates) * jnp.sum(jnp.where(seq_row == numbers, rate, 0.0), axis=0, keepdims=True)

    scaled = []
    for f in range(SIDE):
        weight = jnp.concatenate([sums_over(infos, f, d, own, token_weights) for d in range(SIDE)], axis=0)
        scaled.append((hidden[f].astype(F32) * weight).astype(BF16))
    scaled = jnp.concatenate(scaled, axis=0)

    gradient(0)
    err_pass(2)
    reduce_steps(0)
    gradient(1)
    err_pass(3)
    reduce_steps(1)
    for p in range(2, PASSES):
        gradient(p)
        reduce_steps(p)
    for k in range(CUTS):
        value = own_part(0, k)
        for way in range(2):
            pass_on(way, ring_counts[way] - 1, k).wait_recv()
            value = value + ring_in[way, ring_counts[way] - 1, pl.ds(k * cut, cut)]
        grad[k * cut : (k + 1) * cut] = value

    go.finish()
    for step in range(1, SIDE):
        info_x(step).wait_send()
        info_y(step).wait_send()
        share(0, step).wait_send()
        share(1, step).wait_send()
        home(0, step, 0).wait_send()
        for f in range(SIDE):
            home(1, f, step).wait_send()
    for way, count in ((0, ups), (1, downs)):
        for step in range(count):
            gather(way, step).wait_send()
    for p in range(PASSES):
        for half in range(2):
            twin(p, half).wait_send()
            for step in range(1, SIDE):
                err_first(p, half, step).wait_send()
            for a in range(SIDE):
                for hop in range(1, SIDE):
                    f, d = (hop, a) if half == 0 else (a, hop)
                    err_second(p, half, f, d).wait_send()
    for stage in range(4):
        for step in range(1, stage_sizes[stage]):
            tell(stage, step).wait_send()
    for way in range(2):
        for step in range(ring_counts[way]):
            for k in range(CUTS):
                pass_on(way, step, k).wait_send()


def local(nz, tokens, targets, routes, route_logits, slot_order, seq_ids, w_gate, w_up, w_down):
    tok, feat = tokens.shape
    top = routes.shape[1]
    units = w_gate.shape[2]
    scale = float(tok * lax.axis_size("dp") * lax.axis_size("expert") // 8)
    width = feat // 2

    routes_t, logits_t, order_t = routes.T, route_logits.T, slot_order.T
    slots = lax.broadcasted_iota(jnp.int32, (1, top, 1), 1)
    picked = jnp.sum(jnp.where(order_t[:, None, :] == slots, logits_t[None, :, :], 0.0), axis=1)
    raised = jnp.exp(picked)
    gates = raised / jnp.sum(raised, axis=0, keepdims=True)
    hot = routes_t[None, :, :] == lax.broadcasted_iota(jnp.int32, (EXPERTS, 1, 1), 0)
    named = jnp.sum(jnp.where(hot, 1.0, 0.0), axis=1)
    gate_of = jnp.sum(jnp.where(hot, gates[None], 0.0), axis=1)
    earlier = lax.broadcasted_iota(jnp.int32, (tok, tok), 0) < lax.broadcasted_iota(jnp.int32, (tok, tok), 1)
    ranks = jnp.dot(named.astype(BF16), earlier.astype(BF16), preferred_element_type=F32)
    ranks = jnp.where(named > 0.5, ranks, -1.0)
    seq_rows = jnp.broadcast_to(seq_ids.astype(F32)[None, :], (ROWS_INFO - 2 * EXPERTS, tok))
    info = jnp.concatenate([ranks, gate_of, seq_rows], axis=0)

    vmem = pl.BlockSpec(memory_space=pltpu.VMEM)
    dma = pltpu.SemaphoreType.DMA
    travel = [
        pltpu.VMEM((2, SIDE - 1, tok, width), BF16),
        pltpu.VMEM((2, SIDE, SIDE, CAP, width), BF16),
        pltpu.VMEM((2, SIDE, SIDE, CAP, width), BF16),
    ]
    travel_sems = [
        dma((2, SIDE - 1)), dma((2, SIDE - 1)), dma((2, SIDE, SIDE)), dma((2, SIDE, SIDE)),
    ]
    flops = 2 * EXPERTS * CAP * feat * units
    blocks = feat // LANES
    block = LANES // 2
    per = blocks // (2 * PASSES)
    mixed, grad, losses = pl.pallas_call(
        functools.partial(step_kernel, nz, scale),
        out_shape=(
            jax.ShapeDtypeStruct((tok, feat), BF16),
            jax.ShapeDtypeStruct((block, units), F32),
            jax.ShapeDtypeStruct((8, 2 * NSEQ), F32),
        ),
        in_specs=[vmem] * 6,
        out_specs=[vmem] * 3,
        scratch_shapes=[
            pltpu.VMEM((SIDE, SIDE, ROWS_INFO, tok), F32),
            pltpu.VMEM((SIDE, SIDE * CAP, units), BF16),
            pltpu.VMEM((nz, 2, feat // (2 * nz), units), BF16),
            *travel,
            pltpu.VMEM((2, SIDE, SIDE, CAP, width), BF16),
            pltpu.VMEM((2, SIDE, SIDE, CAP, width), BF16),
            pltpu.VMEM((2, SIDE - 1, tok, width), BF16),
            pltpu.VMEM((2, SIDE - 1, tok, width), BF16),
            pltpu.VMEM((blocks, tok, LANES), BF16),
            pltpu.VMEM((PASSES, 2, SIDE - 1, per, tok, LANES), BF16),
            pltpu.VMEM((PASSES, 2, SIDE, SIDE, CAP, per * LANES), BF16),
            pltpu.VMEM((PASSES, 2, SIDE, SIDE, CAP, per * LANES), BF16),
            pltpu.VMEM((4, 2 * SIDE, 8, 2 * NSEQ), F32),
            pltpu.VMEM((blocks, 2, block, units), F32),
            pltpu.VMEM((blocks, block, units), F32),
            pltpu.VMEM((2, blocks // 2, block, units), F32),
            pltpu.VMEM((2, blocks // 2, block, units), F32),
            dma((2, SIDE - 1)), dma((2, SIDE - 1)),
            *travel_sems,
            dma((2, nz // 2 + 1)), dma((2, nz // 2 + 1)),
            dma((2, SIDE, SIDE)), dma((2, SIDE, SIDE)),
            dma((2, SIDE - 1)), dma((2, SIDE - 1)),
            dma((PASSES, 2, SIDE - 1)), dma((PASSES, 2, SIDE - 1)),
            dma((PASSES, 2, SIDE, SIDE)), dma((PASSES, 2, SIDE, SIDE)),
            dma((4, 2 * SIDE)), dma((4, 2 * SIDE)),
            dma((PASSES, 2)), dma((PASSES, 2)),
            dma((2, blocks // 2, CUTS)), dma((2, blocks // 2, CUTS)),
        ],
        compiler_params=pltpu.CompilerParams(
            collective_id=0, has_side_effects=True, vmem_limit_bytes=60 * 2**20
        ),
        cost_estimate=pl.CostEstimate(flops=4 * flops, bytes_accessed=8 * 2**20, transcendentals=0),
        name="robust_step",
    )(tokens, targets, info, w_gate[0], w_up[0], w_down[:, 0])
    return (mixed, losses[0, :NSEQ], losses[1, :NSEQ], grad[:, None, :])


def solution(mesh):
    return jax.shard_map(
        functools.partial(local, mesh.shape["dp"] // 2),
        mesh=mesh,
        in_specs=(
            P(("dp", "expert"), None),
            P(("dp", "expert"), None),
            P(("dp", "expert"), None),
            P(("dp", "expert"), None),
            P(("dp", "expert"), None),
            P(("dp", "expert")),
            P("expert", None, None),
            P("expert", None, None),
            P("dp", "expert", None),
        ),
        out_specs=(P(("dp", "expert"), None), P(), P(), P("dp", "expert", None)),
        check_vma=False,
    )
```

```python
import functools

import jax
import jax.numpy as jnp
from jax import lax
from jax.experimental import pallas as pl
from jax.experimental.pallas import tpu as pltpu
from jax.sharding import PartitionSpec as P

MESH = pl.DeviceIdType.MESH
SIDE = 4
NSEQ = 64
CAP = 64
EXPERTS = 16
ROWS_INFO = 40
PASSES = 4
CUTS = 2
LANES = 128
F32 = jnp.float32
BF16 = jnp.bfloat16


def position():
    dp, expert = lax.axis_index("dp"), lax.axis_index("expert")
    return dp // 2, dp % 2, expert // SIDE, expert % SIDE


def place(z, core, x, y, dz=0, dx=0, dy=0, nz=1, other=False):
    zz = lax.rem(z + dz + nz, nz) if dz else z
    cc = 1 - core if other else core
    xx = lax.rem(x + dx + SIDE, SIDE)
    yy = lax.rem(y + dy + SIDE, SIDE)
    return {"dp": zz * 2 + cc, "expert": xx * SIDE + yy}


def remote(src, dst, send, recv, device):
    return pltpu.make_async_remote_copy(
        src_ref=src, dst_ref=dst, send_sem=send, recv_sem=recv, device_id=device, device_id_type=MESH
    )


def meet(devices):
    barrier = pltpu.get_barrier_semaphore()
    for device in devices:
        pl.semaphore_signal(barrier, inc=1, device_id=device, device_id_type=MESH)
    pl.semaphore_wait(barrier, len(devices))


def hot_rows(rank_row):
    rows = lax.broadcasted_iota(jnp.int32, (CAP, rank_row.shape[1]), 0).astype(F32)
    return rank_row == rows


def rank_row(infos, f, d, x, y, ef, ed):
    expert = lax.rem(x + ed, SIDE) * SIDE + lax.rem(y + ef, SIDE)
    return infos[f, d, pl.ds(expert, 1), :]


def selection(infos, half, step, x, y):
    parts = []
    for other in range(SIDE):
        if half == 0:
            row = rank_row(infos, 0, step, x, y, other, 0)
        else:
            row = rank_row(infos, step, 0, x, y, 0, other)
        parts.append(hot_rows(row))
    return jnp.where(jnp.concatenate(parts, axis=0), 1.0, 0.0).astype(BF16)


class Dispatch:
    def __init__(self, source, wide, sent, rows, s1, r1, s2, r2, here):
        self.source, self.wide, self.sent, self.rows = source, wide, sent, rows
        self.s1, self.r1, self.s2, self.r2 = s1, r1, s2, r2
        self.here = here
        self.width = source.shape[1] // 2

    def peer(self, half, step):
        return place(*self.here, dx=step) if half == 0 else place(*self.here, dy=step)

    def first(self, half, step):
        src = self.source.at[:, pl.ds(half * self.width, self.width)]
        return remote(
            src, self.wide.at[half, step - 1], self.s1.at[half, step - 1], self.r1.at[half, step - 1],
            self.peer(half, step),
        )

    def second(self, half, f, d):
        hop = f if half == 0 else d
        return remote(
            self.sent.at[half, f, d], self.rows.at[half, f, d], self.s2.at[half, f, d], self.r2.at[half, f, d],
            self.peer(1 - half, hop),
        )

    def late(self, f):
        part = pl.ds(1, SIDE - 1)
        return remote(
            self.sent.at[0, f, part], self.rows.at[0, f, part], self.s2.at[0, f, 1], self.r2.at[0, f, 1], self.peer(1, f)
        )

    def start(self):
        for step in (2, 1, 3):
            for half in range(2):
                self.first(half, step).start()

    def forward(self, infos, half, step, send=True):
        _, _, x, y = self.here
        if step:
            self.first(half, step).wait_recv()
            block = self.wide[half, step - 1]
        else:
            block = self.source[:, half * self.width : (half + 1) * self.width]
        picked = jnp.dot(selection(infos, half, step, x, y), block, preferred_element_type=F32)
        for hop in (2, 1, 3, 0):
            f, d = (hop, step) if half == 0 else (step, hop)
            value = picked[hop * CAP : (hop + 1) * CAP].astype(BF16)
            if hop:
                self.sent[half, f, d] = value
                if send:
                    self.second(half, f, d).start()
            else:
                self.rows[half, f, d] = value

    def arrived(self, f):
        if f:
            self.second(0, f, 0).wait_recv()
            self.late(f).wait_recv()
        for d in range(1, SIDE):
            self.second(1, f, d).wait_recv()

    def finish(self):
        for half in range(2):
            for step in range(1, SIDE):
                self.first(half, step).wait_send()
        for hop in range(1, SIDE):
            self.second(0, hop, 0).wait_send()
            self.late(hop).wait_send()
            for f in range(SIDE):
                self.second(1, f, hop).wait_send()


def dual_search(loss_column):
    lane = lax.broadcasted_iota(jnp.int32, (1, 128), 1).astype(F32)
    upper = jnp.sum(loss_column, axis=0, keepdims=True)
    lower = -upper
    for bits in (7, 7, 7, 7, 7, 5):
        ways = float(2**bits)
        width = (upper - lower) / ways
        middle = lower + width * (lane + 1.0)
        excess = jnp.maximum(loss_column - middle, 0.0)
        plain = jnp.sum(excess, axis=0, keepdims=True)
        square = jnp.sum(excess * excess, axis=0, keepdims=True)
        below = (NSEQ * square - 2.0 * plain * plain < 0.0) & (lane < ways - 1.0)
        count = jnp.sum(jnp.where(below, 1.0, 0.0), axis=1, keepdims=True)
        lower, upper = lower + width * count, lower + width * (count + 1.0)
    return 0.5 * (lower + upper)


def sums_over(infos, f, d, own, values=None):
    ranks, gates = infos[f, d, pl.ds(own, 1), :], infos[f, d, pl.ds(own + EXPERTS, 1), :]
    entry = gates if values is None else values(f, d, gates)
    return jnp.sum(jnp.where(hot_rows(ranks), entry, 0.0), axis=1, keepdims=True)


def column_of(row, size):
    shape = (size, row.shape[1])
    eye = lax.broadcasted_iota(jnp.int32, shape, 0) == lax.broadcasted_iota(jnp.int32, shape, 1)
    return jnp.sum(jnp.where(eye, row, 0.0), axis=1, keepdims=True)


def step_kernel(
    nz, scale, tokens, targets, info, w_gate, w_up, w_down,
    mixed, grad, losses,
    infos, hidden, down, wide, sent, rows, outs, back, part_out, part_in,
    err, err_wide, err_sent, err_rows, seen, grads, twin_in, ring_out, ring_in,
    i_s, i_r, s1, r1, s2, r2, w_s, w_r, b_s, b_r, p_s, p_r,
    e1s, e1r, e2s, e2r, a_s, a_r, t_s, t_r, g_s, g_r,
):
    here = position()
    z, core, x, y = here
    tok, feat = tokens.shape
    width = feat // 2
    own = x * SIDE + y
    ring = lambda dz: place(*here, dz=dz, nz=nz)
    twin_device = place(*here, other=True)
    around = lambda index, step, size: lax.rem(index + step, size)
    stage_sizes = (SIDE, 2 * SIDE, nz)
    stage_index = (x, y * 2 + core, z)
    stages = len(stage_sizes)

    def stage_device(stage, step):
        if stage == 0:
            return place(*here, dx=step)
        if stage == 1:
            to = around(y * 2 + core, step, 2 * SIDE)
            return {"dp": z * 2 + to % 2, "expert": x * SIDE + to // 2}
        return {"dp": around(z, step, nz) * 2 + core, "expert": own}

    peers = [stage_device(stage, step) for stage in range(stages) for step in range(1, stage_sizes[stage])]
    meet(peers)

    infos[0, 0] = info[...]

    def info_x(step):
        return remote(info, infos.at[0, step], i_s.at[0, step - 1], i_r.at[0, step - 1], place(*here, dx=step))

    def info_y(step):
        return remote(info, infos.at[step, 0], i_s.at[1, step - 1], i_r.at[1, step - 1], place(*here, dy=step))

    def info_relay(step):
        part = pl.ds(1, SIDE - 1)
        return remote(
            infos.at[0, part], infos.at[step, part], i_s.at[2, step - 1], i_r.at[2, step - 1], place(*here, dy=step)
        )

    for step in range(1, SIDE):
        info_x(step).start()
        info_y(step).start()
    go = Dispatch(tokens, wide, sent, rows, s1, r1, s2, r2, here)
    go.start()

    ups, downs = nz // 2, nz - 1 - nz // 2

    def gather(way, step):
        block = lax.rem(z - step + nz, nz) if way == 0 else lax.rem(z + step, nz)
        ref = down.at[block, core]
        src = w_down if step == 0 else ref
        return remote(src, ref, w_s.at[way, step], w_r.at[way, step], ring(1 if way == 0 else -1))

    down[z, core] = w_down[...]

    def gather_step(step):
        for way, count in ((0, ups), (1, downs)):
            if 0 < step <= count:
                gather(way, step - 1).wait_recv()
            if step < count:
                gather(way, step).start()

    gather_step(0)
    go.forward(infos, 1, 0)
    go.forward(infos, 0, 0)
    gather_step(1)
    for step in range(1, SIDE):
        info_x(step).wait_recv()
    for step in range(1, SIDE):
        info_relay(step).start()
    gather_step(2)
    tick = 3
    for step in (1, 3, 2):
        go.forward(infos, 0, step, send=False)
        gather_step(tick)
        tick += 1
    for step in range(1, SIDE):
        info_y(step).wait_recv()
    for f in (1, 3, 2):
        go.late(f).start()
        go.forward(infos, 1, f)
        gather_step(tick)
        tick += 1
    for step in range(tick, max(ups, downs) + 1):
        gather_step(step)
    twin_down = [
        remote(down.at[:, side], down.at[:, side], w_s.at[0, ups], w_r.at[0, ups], twin_device) for side in (core, 1 - core)
    ]
    twin_down[0].start()
    for step in range(1, SIDE):
        info_relay(step).wait_recv()

    def home(half, f, d):
        if half == 0:
            return remote(outs.at[0, f], back.at[0, f], b_s.at[0, f, 0], b_r.at[0, f, 0], place(*here, dy=-f))
        return remote(outs.at[1, f, d], back.at[1, f, d], b_s.at[1, f, d], b_r.at[1, f, d], place(*here, dx=-d))

    def expert(f):
        go.arrived(f)
        gate = jnp.zeros((SIDE * CAP, w_gate.shape[1]), F32)
        up = jnp.zeros((SIDE * CAP, w_gate.shape[1]), F32)
        for half in range(2):
            block = rows[half, f].reshape(SIDE * CAP, width)
            gate = gate + jnp.dot(block, w_gate[half * width : (half + 1) * width], preferred_element_type=F32)
            up = up + jnp.dot(block, w_up[half * width : (half + 1) * width], preferred_element_type=F32)
        unit = ((gate / (1.0 + jnp.exp(-gate))) * up).astype(BF16)
        hidden[f] = unit
        weight = jnp.concatenate([sums_over(infos, f, d, own) for d in range(SIDE)], axis=0)
        if f == 0:
            twin_down[0].wait_send()
            twin_down[1].wait_recv()
        for half in range(2):
            matrix = down[half * nz // 2 : (half + 1) * nz // 2].reshape(width, -1)
            value = lax.dot_general(unit, matrix, (((1,), (1,)), ((), ())), preferred_element_type=F32)
            value = (value * weight).astype(BF16).reshape(SIDE, CAP, width)
            if half == 0:
                if f:
                    outs[0, f] = value
                    home(0, f, 0).start()
                else:
                    back[0, 0] = value
            else:
                for d in range(SIDE):
                    if d:
                        outs[1, f, d] = value[d]
                        home(1, f, d).start()
                    else:
                        back[1, f, 0] = value[0]

    def share(half, step):
        device = place(*here, dx=-step) if half == 0 else place(*here, dy=-step)
        return remote(
            part_out.at[half, step - 1], part_in.at[half, step - 1], p_s.at[half, step - 1], p_r.at[half, step - 1], device
        )

    def merge(half, step):
        if half == 0:
            block = back[0, :, step].reshape(SIDE * CAP, width)
        else:
            for d in range(1, SIDE):
                home(1, step, d).wait_recv()
            block = back[1, step].reshape(SIDE * CAP, width)
        total = lax.dot_general(
            selection(infos, half, step, x, y), block, (((0,), (0,)), ((), ())), preferred_element_type=F32
        )
        if step:
            part_out[half, step - 1] = total.astype(BF16)
            share(half, step).start()
        return total

    expert(0)
    expert(1)
    expert(3)
    merge(1, 1)
    expert(2)
    merge(1, 3)
    for f in range(1, SIDE):
        home(0, f, 0).wait_recv()
    for step in (2, 1, 3):
        merge(0, step)
    merge(1, 2)

    blocks = feat // LANES
    squares = jnp.zeros((tok, 1), F32)
    for half in range(2):
        total = merge(half, 0)
        for step in range(1, SIDE):
            share(half, step).wait_recv()
            total = total + part_in[half, step - 1].astype(F32)
        columns = slice(half * width, (half + 1) * width)
        mixed[:, columns] = total.astype(BF16)
        error = total - targets[:, columns].astype(F32)
        low_error = error.astype(BF16)
        for block in range(width // LANES):
            target = half * (width // LANES) + block
            err[lax.rem(target - z + blocks, blocks)] = low_error[:, block * LANES : (block + 1) * LANES]
        squares = squares + jnp.sum(error * error, axis=1, keepdims=True)
    lane = lax.broadcasted_iota(jnp.int32, (tok, 2 * NSEQ), 1)
    number = jnp.where(lane < NSEQ, lane, lane - NSEQ).astype(F32)
    entry = jnp.where(lane < NSEQ, squares, 1.0)
    seq_column = column_of(info[2 * EXPERTS : 2 * EXPERTS + 1, :], tok)
    partial = jnp.sum(jnp.where(seq_column == number, entry, 0.0), axis=0, keepdims=True)

    def tell(stage, step):
        slot = seen.at[stage, stage_index[stage]]
        return remote(slot, slot, a_s.at[stage, step - 1], a_r.at[stage, step - 1], stage_device(stage, step))

    def stage_start(stage, value):
        seen[stage, stage_index[stage]] = value
        for step in range(1, stage_sizes[stage]):
            tell(stage, step).start()

    def stage_end(stage):
        for step in range(1, stage_sizes[stage]):
            tell(stage, step).wait_recv()
        value = seen[stage, 0]
        for index in range(1, stage_sizes[stage]):
            value = value + seen[stage, index]
        if stage + 1 < stages:
            stage_start(stage + 1, value)
        return value

    stage_start(0, jnp.broadcast_to(partial, (8, 2 * NSEQ)))

    per = blocks // (2 * PASSES)

    def span(half, p):
        return blocks // 2 - per * (p + 1) if half == 0 else blocks // 2 + per * p

    def err_first(p, half, step):
        device = place(*here, dx=step) if half == 0 else place(*here, dy=step)
        return remote(
            err.at[pl.ds(span(half, p), per)], err_wide.at[p, half, step - 1],
            e1s.at[p, half, step - 1], e1r.at[p, half, step - 1], device,
        )

    def err_second(p, half, hop, late):
        device = place(*here, dy=hop) if half == 0 else place(*here, dx=hop)
        part = pl.ds(0, SIDE)
        if p == 0:
            part = pl.ds(1, SIDE - 1) if late else pl.ds(0, 1)
        return remote(
            err_sent.at[p, half, hop, part], err_rows.at[p, half, hop, part],
            e2s.at[p, half, hop, late], e2r.at[p, half, hop, late], device,
        )

    def err_start(p):
        for step in (2, 1, 3):
            for half in range(2):
                err_first(p, half, step).start()

    def err_forward(p, half, step):
        if step:
            err_first(p, half, step).wait_recv()
            block = jnp.concatenate([err_wide[p, half, step - 1, i] for i in range(per)], axis=1)
        else:
            block = jnp.concatenate([err[span(half, p) + i] for i in range(per)], axis=1)
        picked = jnp.dot(selection(infos, half, step, x, y), block, preferred_element_type=F32)
        for hop in (2, 1, 3, 0):
            value = picked[hop * CAP : (hop + 1) * CAP].astype(BF16)
            if hop:
                err_sent[p, half, hop, step] = value
                if step == 2 or (p == 0 and step == 0):
                    err_second(p, half, hop, int(step == 2)).start()
            else:
                err_rows[p, half, 0, step] = value

    def err_arrived(p):
        for half in range(2):
            for hop in range(1, SIDE):
                for late in range(1 if p else 0, 2):
                    err_second(p, half, hop, late).wait_recv()

    block_rows = LANES // 2

    def twin(p, half):
        ref = pl.ds(span(half, p), per)
        return remote(grads.at[ref, 1 - core], twin_in.at[ref], t_s.at[p, half], t_r.at[p, half], twin_device)

    def gradient(p):
        err_arrived(p)
        for half in range(2):
            if half == 0:
                block = err_rows[p, 0].reshape(SIDE * SIDE * CAP, per * LANES)
            else:
                block = jnp.concatenate(
                    [err_rows[p, 1, :, f].reshape(SIDE * CAP, per * LANES) for f in range(SIDE)], axis=0
                )
            value = lax.dot_general(
                block, scaled,
                (((0,), (0,)), ((), ())), preferred_element_type=F32,
            )
            grads[span(half, p) : span(half, p) + per] = value.reshape(per, 2, block_rows, -1)
            twin(p, half).start()

    cut = block_rows // CUTS
    ring_counts = (blocks // 2 - 1, blocks // 2)

    def pass_on(way, step, k):
        part = pl.ds(k * cut, cut)
        return remote(
            ring_out.at[way, step, part], ring_in.at[way, step, part], g_s.at[way, step, k], g_r.at[way, step, k],
            ring(1 if way == 0 else -1),
        )

    def own_part(block, k):
        part = pl.ds(k * cut, cut)
        return grads[block, core, part] + twin_in[block, part]

    def reduce_steps(p):
        for half in range(2):
            twin(p, half).wait_recv()
        for step in range(per * p, per * (p + 1)):
            for k in range(CUTS):
                for way in range(2):
                    if step < ring_counts[way]:
                        block = blocks // 2 - 1 - step if way == 0 else blocks // 2 + step
                        value = own_part(block, k)
                        if step:
                            pass_on(way, step - 1, k).wait_recv()
                            value = value + ring_in[way, step - 1, pl.ds(k * cut, cut)]
                        ring_out[way, step, pl.ds(k * cut, cut)] = value
                        pass_on(way, step, k).start()

    def err_both(p, *steps):
        for step in steps:
            for half in range(2):
                err_forward(p, half, step)

    err_start(0)
    err_both(0, 0)
    err_start(1)
    err_both(0, 1)
    stage_end(0)
    err_both(0, 3, 2)
    stage_end(1)
    err_both(1, 0)
    err_start(2)
    err_both(1, 1, 3, 2)
    sums = stage_end(2)[0:1]
    err_start(3)
    lengths = pltpu.roll(sums, NSEQ, 1)
    loss_row = sums / (lengths * float(feat))
    loss_column = column_of(loss_row, NSEQ)
    eta = dual_search(loss_column)
    excess_column = jnp.maximum(loss_column - eta, 0.0)
    norm = jnp.sum(excess_column, axis=0, keepdims=True)
    losses[0:1, :] = loss_row
    losses[1:2, :] = jnp.maximum(loss_row - eta, 0.0) / norm
    rate = (excess_column / norm) / column_of(lengths, NSEQ)
    numbers = lax.broadcasted_iota(jnp.int32, (NSEQ, tok), 0).astype(F32)

    def token_weights(f, d, gates):
        seq_row = infos[f, d, 2 * EXPERTS : 2 * EXPERTS + 1, :]
        return (scale * gates) * jnp.sum(jnp.where(seq_row == numbers, rate, 0.0), axis=0, keepdims=True)

    scaled = []
    for f in range(SIDE):
        weight = jnp.concatenate([sums_over(infos, f, d, own, token_weights) for d in range(SIDE)], axis=0)
        scaled.append((hidden[f].astype(F32) * weight).astype(BF16))
    scaled = jnp.concatenate(scaled, axis=0)

    gradient(0)
    err_both(2, 0, 1, 3, 2)
    reduce_steps(0)
    gradient(1)
    err_both(3, 0, 1, 3, 2)
    reduce_steps(1)
    for p in range(2, PASSES):
        gradient(p)
        reduce_steps(p)
    for k in range(CUTS):
        value = own_part(0, k)
        for way in range(2):
            pass_on(way, ring_counts[way] - 1, k).wait_recv()
            value = value + ring_in[way, ring_counts[way] - 1, pl.ds(k * cut, cut)]
        grad[k * cut : (k + 1) * cut] = value

    go.finish()
    for step in range(1, SIDE):
        info_x(step).wait_send()
        info_y(step).wait_send()
        info_relay(step).wait_send()
        share(0, step).wait_send()
        share(1, step).wait_send()
        home(0, step, 0).wait_send()
        for f in range(SIDE):
            home(1, f, step).wait_send()
    for way, count in ((0, ups), (1, downs)):
        for step in range(count):
            gather(way, step).wait_send()
    for p in range(PASSES):
        for half in range(2):
            twin(p, half).wait_send()
            for step in range(1, SIDE):
                err_first(p, half, step).wait_send()
            for hop in range(1, SIDE):
                for late in range(1 if p else 0, 2):
                    err_second(p, half, hop, late).wait_send()
    for stage in range(stages):
        for step in range(1, stage_sizes[stage]):
            tell(stage, step).wait_send()
    for way in range(2):
        for step in range(ring_counts[way]):
            for k in range(CUTS):
                pass_on(way, step, k).wait_send()


def local(nz, tokens, targets, routes, route_logits, slot_order, seq_ids, w_gate, w_up, w_down):
    tok, feat = tokens.shape
    top = routes.shape[1]
    units = w_gate.shape[2]
    scale = float(tok * lax.axis_size("dp") * lax.axis_size("expert") // 8)
    width = feat // 2

    routes_t, logits_t, order_t = routes.T, route_logits.T, slot_order.T
    slots = lax.broadcasted_iota(jnp.int32, (1, top, 1), 1)
    picked = jnp.sum(jnp.where(order_t[:, None, :] == slots, logits_t[None, :, :], 0.0), axis=1)
    raised = jnp.exp(picked)
    gates = raised / jnp.sum(raised, axis=0, keepdims=True)
    hot = routes_t[None, :, :] == lax.broadcasted_iota(jnp.int32, (EXPERTS, 1, 1), 0)
    named = jnp.sum(jnp.where(hot, 1.0, 0.0), axis=1)
    gate_of = jnp.sum(jnp.where(hot, gates[None], 0.0), axis=1)
    earlier = lax.broadcasted_iota(jnp.int32, (tok, tok), 0) < lax.broadcasted_iota(jnp.int32, (tok, tok), 1)
    ranks = jnp.dot(named.astype(BF16), earlier.astype(BF16), preferred_element_type=F32)
    ranks = jnp.where(named > 0.5, ranks, -1.0)
    seq_rows = jnp.broadcast_to(seq_ids.astype(F32)[None, :], (ROWS_INFO - 2 * EXPERTS, tok))
    info = jnp.concatenate([ranks, gate_of, seq_rows], axis=0)

    vmem = pl.BlockSpec(memory_space=pltpu.VMEM)
    dma = pltpu.SemaphoreType.DMA
    travel = [
        pltpu.VMEM((2, SIDE - 1, tok, width), BF16),
        pltpu.VMEM((2, SIDE, SIDE, CAP, width), BF16),
        pltpu.VMEM((2, SIDE, SIDE, CAP, width), BF16),
    ]
    travel_sems = [
        dma((2, SIDE - 1)), dma((2, SIDE - 1)), dma((2, SIDE, SIDE)), dma((2, SIDE, SIDE)),
    ]
    flops = 2 * EXPERTS * CAP * feat * units
    blocks = feat // LANES
    block = LANES // 2
    per = blocks // (2 * PASSES)
    mixed, grad, losses = pl.pallas_call(
        functools.partial(step_kernel, nz, scale),
        out_shape=(
            jax.ShapeDtypeStruct((tok, feat), BF16),
            jax.ShapeDtypeStruct((block, units), F32),
            jax.ShapeDtypeStruct((8, 2 * NSEQ), F32),
        ),
        in_specs=[vmem] * 6,
        out_specs=[vmem] * 3,
        scratch_shapes=[
            pltpu.VMEM((SIDE, SIDE, ROWS_INFO, tok), F32),
            pltpu.VMEM((SIDE, SIDE * CAP, units), BF16),
            pltpu.VMEM((nz, 2, feat // (2 * nz), units), BF16),
            *travel,
            pltpu.VMEM((2, SIDE, SIDE, CAP, width), BF16),
            pltpu.VMEM((2, SIDE, SIDE, CAP, width), BF16),
            pltpu.VMEM((2, SIDE - 1, tok, width), BF16),
            pltpu.VMEM((2, SIDE - 1, tok, width), BF16),
            pltpu.VMEM((blocks, tok, LANES), BF16),
            pltpu.VMEM((PASSES, 2, SIDE - 1, per, tok, LANES), BF16),
            pltpu.VMEM((PASSES, 2, SIDE, SIDE, CAP, per * LANES), BF16),
            pltpu.VMEM((PASSES, 2, SIDE, SIDE, CAP, per * LANES), BF16),
            pltpu.VMEM((3, max(2 * SIDE, nz), 8, 2 * NSEQ), F32),
            pltpu.VMEM((blocks, 2, block, units), F32),
            pltpu.VMEM((blocks, block, units), F32),
            pltpu.VMEM((2, blocks // 2, block, units), F32),
            pltpu.VMEM((2, blocks // 2, block, units), F32),
            dma((3, SIDE - 1)), dma((3, SIDE - 1)),
            *travel_sems,
            dma((2, nz // 2 + 1)), dma((2, nz // 2 + 1)),
            dma((2, SIDE, SIDE)), dma((2, SIDE, SIDE)),
            dma((2, SIDE - 1)), dma((2, SIDE - 1)),
            dma((PASSES, 2, SIDE - 1)), dma((PASSES, 2, SIDE - 1)),
            dma((PASSES, 2, SIDE, 2)), dma((PASSES, 2, SIDE, 2)),
            dma((3, max(2 * SIDE, nz))), dma((3, max(2 * SIDE, nz))),
            dma((PASSES, 2)), dma((PASSES, 2)),
            dma((2, blocks // 2, CUTS)), dma((2, blocks // 2, CUTS)),
        ],
        compiler_params=pltpu.CompilerParams(
            collective_id=0, has_side_effects=True, vmem_limit_bytes=60 * 2**20
        ),
        cost_estimate=pl.CostEstimate(flops=4 * flops, bytes_accessed=8 * 2**20, transcendentals=0),
        name="robust_step",
    )(tokens, targets, info, w_gate[0], w_up[0], w_down[:, 0])
    return (mixed, losses[0, :NSEQ], losses[1, :NSEQ], grad[:, None, :])


def solution(mesh):
    return jax.shard_map(
        functools.partial(local, mesh.shape["dp"] // 2),
        mesh=mesh,
        in_specs=(
            P(("dp", "expert"), None),
            P(("dp", "expert"), None),
            P(("dp", "expert"), None),
            P(("dp", "expert"), None),
            P(("dp", "expert"), None),
            P(("dp", "expert")),
            P("expert", None, None),
            P("expert", None, None),
            P("dp", "expert", None),
        ),
        out_specs=(P(("dp", "expert"), None), P(), P(), P("dp", "expert", None)),
        check_vma=False,
    )
```

```python
import functools

import jax
import jax.numpy as jnp
from jax import lax
from jax.experimental import pallas as pl
from jax.experimental.pallas import tpu as pltpu
from jax.sharding import PartitionSpec as P

MESH = pl.DeviceIdType.MESH
SIDE = 4
NSEQ = 64
CAP = 64
EXPERTS = 16
ROWS_INFO = 40
PASSES = 4
CUTS = 2
LANES = 128
F32 = jnp.float32
BF16 = jnp.bfloat16


def position():
    dp, expert = lax.axis_index("dp"), lax.axis_index("expert")
    return dp // 2, dp % 2, expert // SIDE, expert % SIDE


def place(z, core, x, y, dz=0, dx=0, dy=0, nz=1, other=False):
    zz = lax.rem(z + dz + nz, nz) if dz else z
    cc = 1 - core if other else core
    xx = lax.rem(x + dx + SIDE, SIDE)
    yy = lax.rem(y + dy + SIDE, SIDE)
    return {"dp": zz * 2 + cc, "expert": xx * SIDE + yy}


def remote(src, dst, send, recv, device):
    return pltpu.make_async_remote_copy(
        src_ref=src, dst_ref=dst, send_sem=send, recv_sem=recv, device_id=device, device_id_type=MESH
    )


def meet(devices, meanwhile):
    barrier = pltpu.get_barrier_semaphore()
    for device in devices:
        pl.semaphore_signal(barrier, inc=1, device_id=device, device_id_type=MESH)
    meanwhile()
    pl.semaphore_wait(barrier, len(devices))


def routing(routes, logits, order, seq_ids, info):
    top, tok = routes.shape
    slots = lax.broadcasted_iota(jnp.int32, (top, tok), 0)
    experts = lax.broadcasted_iota(jnp.int32, (EXPERTS, tok), 0)
    named = jnp.zeros((EXPERTS, tok), F32)
    gates = jnp.zeros((EXPERTS, tok), F32)
    for k in range(top):
        score = jnp.sum(jnp.where(order[k : k + 1, :] == slots, logits[...], 0.0), axis=0, keepdims=True)
        hot = routes[k : k + 1, :] == experts
        named = jnp.where(hot, 1.0, named)
        gates = jnp.where(hot, jnp.exp(score), gates)
    gates = gates / jnp.sum(gates, axis=0, keepdims=True)
    earlier = lax.broadcasted_iota(jnp.int32, (tok, tok), 0) < lax.broadcasted_iota(jnp.int32, (tok, tok), 1)
    ranks = jnp.dot(named.astype(BF16), jnp.where(earlier, 1.0, 0.0).astype(BF16), preferred_element_type=F32)
    info[0:EXPERTS, :] = jnp.where(named > 0.5, ranks, -1.0)
    info[EXPERTS : 2 * EXPERTS, :] = gates
    info[2 * EXPERTS :, :] = jnp.broadcast_to(seq_ids[...].astype(F32), (ROWS_INFO - 2 * EXPERTS, tok))


def hot_rows(rank_row):
    rows = lax.broadcasted_iota(jnp.int32, (CAP, rank_row.shape[1]), 0).astype(F32)
    return rank_row == rows


def rank_row(infos, f, d, x, y, ef, ed):
    expert = lax.rem(x + ed, SIDE) * SIDE + lax.rem(y + ef, SIDE)
    return infos[f, d, pl.ds(expert, 1), :]


def selection(infos, half, step, x, y):
    parts = []
    for other in range(SIDE):
        if half == 0:
            row = rank_row(infos, 0, step, x, y, other, 0)
        else:
            row = rank_row(infos, step, 0, x, y, 0, other)
        parts.append(hot_rows(row))
    return jnp.where(jnp.concatenate(parts, axis=0), 1.0, 0.0).astype(BF16)


class Dispatch:
    def __init__(self, source, wide, sent, rows, s1, r1, s2, r2, here):
        self.source, self.wide, self.sent, self.rows = source, wide, sent, rows
        self.s1, self.r1, self.s2, self.r2 = s1, r1, s2, r2
        self.here = here
        self.width = source.shape[1] // 2

    def peer(self, half, step):
        return place(*self.here, dx=step) if half == 0 else place(*self.here, dy=step)

    def first(self, half, step):
        src = self.source.at[:, pl.ds(half * self.width, self.width)]
        return remote(
            src, self.wide.at[half, step - 1], self.s1.at[half, step - 1], self.r1.at[half, step - 1],
            self.peer(half, step),
        )

    def second(self, half, f, d):
        hop = f if half == 0 else d
        return remote(
            self.sent.at[half, f, d], self.rows.at[half, f, d], self.s2.at[half, f, d], self.r2.at[half, f, d],
            self.peer(1 - half, hop),
        )

    def late(self, f):
        part = pl.ds(1, SIDE - 1)
        return remote(
            self.sent.at[0, f, part], self.rows.at[0, f, part], self.s2.at[0, f, 1], self.r2.at[0, f, 1], self.peer(1, f)
        )

    def start(self):
        for step in (2, 1, 3):
            for half in range(2):
                self.first(half, step).start()

    def forward(self, infos, half, step, send=True):
        _, _, x, y = self.here
        if step:
            self.first(half, step).wait_recv()
            block = self.wide[half, step - 1]
        else:
            block = self.source[:, half * self.width : (half + 1) * self.width]
        picked = jnp.dot(selection(infos, half, step, x, y), block, preferred_element_type=F32)
        for hop in (2, 1, 3, 0):
            f, d = (hop, step) if half == 0 else (step, hop)
            value = picked[hop * CAP : (hop + 1) * CAP].astype(BF16)
            if hop:
                self.sent[half, f, d] = value
                if send:
                    self.second(half, f, d).start()
            else:
                self.rows[half, f, d] = value

    def arrived(self, f):
        if f:
            self.second(0, f, 0).wait_recv()
            self.late(f).wait_recv()
        for d in range(1, SIDE):
            self.second(1, f, d).wait_recv()

    def finish(self):
        for half in range(2):
            for step in range(1, SIDE):
                self.first(half, step).wait_send()
        for hop in range(1, SIDE):
            self.second(0, hop, 0).wait_send()
            self.late(hop).wait_send()
            for f in range(SIDE):
                self.second(1, f, hop).wait_send()


def dual_search(loss_column):
    lane = lax.broadcasted_iota(jnp.int32, (1, 128), 1).astype(F32)
    upper = jnp.sum(loss_column, axis=0, keepdims=True)
    lower = -upper
    for bits in (7, 7, 7, 7, 7, 5):
        ways = float(2**bits)
        width = (upper - lower) / ways
        middle = lower + width * (lane + 1.0)
        excess = jnp.maximum(loss_column - middle, 0.0)
        plain = jnp.sum(excess, axis=0, keepdims=True)
        square = jnp.sum(excess * excess, axis=0, keepdims=True)
        below = (NSEQ * square - 2.0 * plain * plain < 0.0) & (lane < ways - 1.0)
        count = jnp.sum(jnp.where(below, 1.0, 0.0), axis=1, keepdims=True)
        lower, upper = lower + width * count, lower + width * (count + 1.0)
    return 0.5 * (lower + upper)


def sums_over(infos, f, d, own, values=None):
    ranks, gates = infos[f, d, pl.ds(own, 1), :], infos[f, d, pl.ds(own + EXPERTS, 1), :]
    entry = gates if values is None else values(f, d, gates)
    return jnp.sum(jnp.where(hot_rows(ranks), entry, 0.0), axis=1, keepdims=True)


def column_of(row, size):
    shape = (size, row.shape[1])
    eye = lax.broadcasted_iota(jnp.int32, shape, 0) == lax.broadcasted_iota(jnp.int32, shape, 1)
    return jnp.sum(jnp.where(eye, row, 0.0), axis=1, keepdims=True)


def step_kernel(
    nz, scale, tokens, targets, routes, route_logits, slot_order, seq_ids, w_gate, w_up, w_down,
    mixed, grad, losses,
    info, infos, hidden, down, wide, sent, rows, outs, back, part_out, part_in,
    err, err_wide, err_sent, err_rows, seen, grads, twin_in, ring_out, ring_in,
    i_s, i_r, s1, r1, s2, r2, w_s, w_r, b_s, b_r, p_s, p_r,
    e1s, e1r, e2s, e2r, a_s, a_r, t_s, t_r, g_s, g_r,
):
    here = position()
    z, core, x, y = here
    tok, feat = tokens.shape
    width = feat // 2
    own = x * SIDE + y
    ring = lambda dz: place(*here, dz=dz, nz=nz)
    twin_device = place(*here, other=True)
    around = lambda index, step, size: lax.rem(index + step, size)
    stage_sizes = (SIDE, 2 * SIDE, nz)
    stage_index = (x, y * 2 + core, z)
    stages = len(stage_sizes)

    def stage_device(stage, step):
        if stage == 0:
            return place(*here, dx=step)
        if stage == 1:
            to = around(y * 2 + core, step, 2 * SIDE)
            return {"dp": z * 2 + to % 2, "expert": x * SIDE + to // 2}
        return {"dp": around(z, step, nz) * 2 + core, "expert": own}

    peers = [stage_device(stage, step) for stage in range(stages) for step in range(1, stage_sizes[stage])]
    meet(peers, lambda: routing(routes, route_logits, slot_order, seq_ids, info))

    infos[0, 0] = info[...]

    def info_x(step):
        return remote(info, infos.at[0, step], i_s.at[0, step - 1], i_r.at[0, step - 1], place(*here, dx=step))

    def info_y(step):
        return remote(info, infos.at[step, 0], i_s.at[1, step - 1], i_r.at[1, step - 1], place(*here, dy=step))

    def info_relay(step):
        part = pl.ds(1, SIDE - 1)
        return remote(
            infos.at[0, part], infos.at[step, part], i_s.at[2, step - 1], i_r.at[2, step - 1], place(*here, dy=step)
        )

    for step in range(1, SIDE):
        info_x(step).start()
        info_y(step).start()
    go = Dispatch(tokens, wide, sent, rows, s1, r1, s2, r2, here)
    go.start()

    ups, downs = nz // 2, nz - 1 - nz // 2

    def gather(way, step):
        block = lax.rem(z - step + nz, nz) if way == 0 else lax.rem(z + step, nz)
        ref = down.at[block, core]
        src = w_down if step == 0 else ref
        return remote(src, ref, w_s.at[way, step], w_r.at[way, step], ring(1 if way == 0 else -1))

    down[z, core] = w_down[...]

    def gather_step(step):
        for way, count in ((0, ups), (1, downs)):
            if 0 < step <= count:
                gather(way, step - 1).wait_recv()
            if step < count:
                gather(way, step).start()

    gather_step(0)
    go.forward(infos, 1, 0)
    go.forward(infos, 0, 0)
    gather_step(1)
    for step in range(1, SIDE):
        info_x(step).wait_recv()
    for step in range(1, SIDE):
        info_relay(step).start()
    gather_step(2)
    tick = 3
    for step in (1, 3, 2):
        go.forward(infos, 0, step, send=False)
        gather_step(tick)
        tick += 1
    for step in range(1, SIDE):
        info_y(step).wait_recv()
    for f in (1, 3, 2):
        go.late(f).start()
        go.forward(infos, 1, f)
        gather_step(tick)
        tick += 1
    for step in range(tick, max(ups, downs) + 1):
        gather_step(step)
    twin_down = [
        remote(down.at[:, side], down.at[:, side], w_s.at[0, ups], w_r.at[0, ups], twin_device) for side in (core, 1 - core)
    ]
    twin_down[0].start()
    for step in range(1, SIDE):
        info_relay(step).wait_recv()

    def home(half, f, d):
        if half == 0:
            return remote(outs.at[0, f], back.at[0, f], b_s.at[0, f, 0], b_r.at[0, f, 0], place(*here, dy=-f))
        return remote(outs.at[1, f, d], back.at[1, f, d], b_s.at[1, f, d], b_r.at[1, f, d], place(*here, dx=-d))

    def expert(f):
        go.arrived(f)
        gate = jnp.zeros((SIDE * CAP, w_gate.shape[1]), F32)
        up = jnp.zeros((SIDE * CAP, w_gate.shape[1]), F32)
        for half in range(2):
            block = rows[half, f].reshape(SIDE * CAP, width)
            gate = gate + jnp.dot(block, w_gate[half * width : (half + 1) * width], preferred_element_type=F32)
            up = up + jnp.dot(block, w_up[half * width : (half + 1) * width], preferred_element_type=F32)
        unit = ((gate / (1.0 + jnp.exp(-gate))) * up).astype(BF16)
        hidden[f] = unit
        weight = jnp.concatenate([sums_over(infos, f, d, own) for d in range(SIDE)], axis=0)
        if f == 0:
            twin_down[0].wait_send()
            twin_down[1].wait_recv()
        for half in range(2):
            matrix = down[half * nz // 2 : (half + 1) * nz // 2].reshape(width, -1)
            value = lax.dot_general(unit, matrix, (((1,), (1,)), ((), ())), preferred_element_type=F32)
            value = (value * weight).astype(BF16).reshape(SIDE, CAP, width)
            if half == 0:
                if f:
                    outs[0, f] = value
                    home(0, f, 0).start()
                else:
                    back[0, 0] = value
            else:
                for d in range(SIDE):
                    if d:
                        outs[1, f, d] = value[d]
                        home(1, f, d).start()
                    else:
                        back[1, f, 0] = value[0]

    def share(half, step):
        device = place(*here, dx=-step) if half == 0 else place(*here, dy=-step)
        return remote(
            part_out.at[half, step - 1], part_in.at[half, step - 1], p_s.at[half, step - 1], p_r.at[half, step - 1], device
        )

    def merge(half, step):
        if half == 0:
            block = back[0, :, step].reshape(SIDE * CAP, width)
        else:
            for d in range(1, SIDE):
                home(1, step, d).wait_recv()
            block = back[1, step].reshape(SIDE * CAP, width)
        total = lax.dot_general(
            selection(infos, half, step, x, y), block, (((0,), (0,)), ((), ())), preferred_element_type=F32
        )
        if step:
            part_out[half, step - 1] = total.astype(BF16)
            share(half, step).start()
        return total

    expert(0)
    expert(1)
    expert(3)
    merge(1, 1)
    expert(2)
    merge(1, 3)
    for f in range(1, SIDE):
        home(0, f, 0).wait_recv()
    for step in (2, 1, 3):
        merge(0, step)
    merge(1, 2)

    blocks = feat // LANES
    squares = jnp.zeros((tok, 1), F32)
    for half in range(2):
        total = merge(half, 0)
        for step in range(1, SIDE):
            share(half, step).wait_recv()
            total = total + part_in[half, step - 1].astype(F32)
        columns = slice(half * width, (half + 1) * width)
        mixed[:, columns] = total.astype(BF16)
        error = total - targets[:, columns].astype(F32)
        low_error = error.astype(BF16)
        for block in range(width // LANES):
            target = half * (width // LANES) + block
            err[lax.rem(target - z + blocks, blocks)] = low_error[:, block * LANES : (block + 1) * LANES]
        squares = squares + jnp.sum(error * error, axis=1, keepdims=True)
    lane = lax.broadcasted_iota(jnp.int32, (tok, 2 * NSEQ), 1)
    number = jnp.where(lane < NSEQ, lane, lane - NSEQ).astype(F32)
    entry = jnp.where(lane < NSEQ, squares, 1.0)
    seq_column = column_of(info[2 * EXPERTS : 2 * EXPERTS + 1, :], tok)
    partial = jnp.sum(jnp.where(seq_column == number, entry, 0.0), axis=0, keepdims=True)

    def tell(stage, step):
        slot = seen.at[stage, stage_index[stage]]
        return remote(slot, slot, a_s.at[stage, step - 1], a_r.at[stage, step - 1], stage_device(stage, step))

    def stage_start(stage, value):
        seen[stage, stage_index[stage]] = value
        for step in range(1, stage_sizes[stage]):
            tell(stage, step).start()

    def stage_end(stage):
        for step in range(1, stage_sizes[stage]):
            tell(stage, step).wait_recv()
        value = seen[stage, 0]
        for index in range(1, stage_sizes[stage]):
            value = value + seen[stage, index]
        if stage + 1 < stages:
            stage_start(stage + 1, value)
        return value

    stage_start(0, jnp.broadcast_to(partial, (8, 2 * NSEQ)))

    per = blocks // (2 * PASSES)

    def span(half, p):
        return blocks // 2 - per * (p + 1) if half == 0 else blocks // 2 + per * p

    def err_first(p, half, step):
        device = place(*here, dx=step) if half == 0 else place(*here, dy=step)
        return remote(
            err.at[pl.ds(span(half, p), per)], err_wide.at[p, half, step - 1],
            e1s.at[p, half, step - 1], e1r.at[p, half, step - 1], device,
        )

    def err_second(p, half, hop, late):
        device = place(*here, dy=hop) if half == 0 else place(*here, dx=hop)
        part = pl.ds(0, SIDE)
        if p == 0:
            part = pl.ds(1, SIDE - 1) if late else pl.ds(0, 1)
        return remote(
            err_sent.at[p, half, hop, part], err_rows.at[p, half, hop, part],
            e2s.at[p, half, hop, late], e2r.at[p, half, hop, late], device,
        )

    def err_start(p):
        for step in (2, 1, 3):
            for half in range(2):
                err_first(p, half, step).start()

    def err_forward(p, half, step):
        if step:
            err_first(p, half, step).wait_recv()
            block = jnp.concatenate([err_wide[p, half, step - 1, i] for i in range(per)], axis=1)
        else:
            block = jnp.concatenate([err[span(half, p) + i] for i in range(per)], axis=1)
        picked = jnp.dot(selection(infos, half, step, x, y), block, preferred_element_type=F32)
        for hop in (2, 1, 3, 0):
            value = picked[hop * CAP : (hop + 1) * CAP].astype(BF16)
            if hop:
                err_sent[p, half, hop, step] = value
                if step == 2 or (p == 0 and step == 0):
                    err_second(p, half, hop, int(step == 2)).start()
            else:
                err_rows[p, half, 0, step] = value

    def err_arrived(p):
        for half in range(2):
            for hop in range(1, SIDE):
                for late in range(1 if p else 0, 2):
                    err_second(p, half, hop, late).wait_recv()

    block_rows = LANES // 2

    def twin(p, half):
        ref = pl.ds(span(half, p), per)
        return remote(grads.at[ref, 1 - core], twin_in.at[ref], t_s.at[p, half], t_r.at[p, half], twin_device)

    def gradient(p):
        err_arrived(p)
        for half in range(2):
            if half == 0:
                block = err_rows[p, 0].reshape(SIDE * SIDE * CAP, per * LANES)
            else:
                block = jnp.concatenate(
                    [err_rows[p, 1, :, f].reshape(SIDE * CAP, per * LANES) for f in range(SIDE)], axis=0
                )
            value = lax.dot_general(
                block, scaled,
                (((0,), (0,)), ((), ())), preferred_element_type=F32,
            )
            grads[span(half, p) : span(half, p) + per] = value.reshape(per, 2, block_rows, -1)
            twin(p, half).start()

    cut = block_rows // CUTS
    ring_counts = (blocks // 2 - 1, blocks // 2)

    def pass_on(way, step, k):
        part = pl.ds(k * cut, cut)
        return remote(
            ring_out.at[way, step, part], ring_in.at[way, step, part], g_s.at[way, step, k], g_r.at[way, step, k],
            ring(1 if way == 0 else -1),
        )

    def own_part(block, k):
        part = pl.ds(k * cut, cut)
        return grads[block, core, part] + twin_in[block, part]

    def reduce_steps(p):
        for half in range(2):
            twin(p, half).wait_recv()
        for step in range(per * p, per * (p + 1)):
            for k in range(CUTS):
                for way in range(2):
                    if step < ring_counts[way]:
                        block = blocks // 2 - 1 - step if way == 0 else blocks // 2 + step
                        value = own_part(block, k)
                        if step:
                            pass_on(way, step - 1, k).wait_recv()
                            value = value + ring_in[way, step - 1, pl.ds(k * cut, cut)]
                        ring_out[way, step, pl.ds(k * cut, cut)] = value
                        pass_on(way, step, k).start()

    def err_both(p, *steps):
        for step in steps:
            for half in range(2):
                err_forward(p, half, step)

    err_start(0)
    err_both(0, 0)
    err_start(1)
    err_both(0, 1)
    stage_end(0)
    err_both(0, 3, 2)
    stage_end(1)
    err_both(1, 0)
    err_start(2)
    err_both(1, 1, 3, 2)
    sums = stage_end(2)[0:1]
    err_start(3)
    lengths = pltpu.roll(sums, NSEQ, 1)
    loss_row = sums / (lengths * float(feat))
    loss_column = column_of(loss_row, NSEQ)
    eta = dual_search(loss_column)
    excess_column = jnp.maximum(loss_column - eta, 0.0)
    norm = jnp.sum(excess_column, axis=0, keepdims=True)
    losses[0:1, :] = loss_row
    losses[1:2, :] = jnp.maximum(loss_row - eta, 0.0) / norm
    rate = (excess_column / norm) / column_of(lengths, NSEQ)
    numbers = lax.broadcasted_iota(jnp.int32, (NSEQ, tok), 0).astype(F32)

    def token_weights(f, d, gates):
        seq_row = infos[f, d, 2 * EXPERTS : 2 * EXPERTS + 1, :]
        return (scale * gates) * jnp.sum(jnp.where(seq_row == numbers, rate, 0.0), axis=0, keepdims=True)

    scaled = []
    for f in range(SIDE):
        weight = jnp.concatenate([sums_over(infos, f, d, own, token_weights) for d in range(SIDE)], axis=0)
        scaled.append((hidden[f].astype(F32) * weight).astype(BF16))
    scaled = jnp.concatenate(scaled, axis=0)

    gradient(0)
    err_both(2, 0, 1, 3, 2)
    reduce_steps(0)
    gradient(1)
    err_both(3, 0, 1, 3, 2)
    reduce_steps(1)
    for p in range(2, PASSES):
        gradient(p)
        reduce_steps(p)
    for k in range(CUTS):
        value = own_part(0, k)
        for way in range(2):
            pass_on(way, ring_counts[way] - 1, k).wait_recv()
            value = value + ring_in[way, ring_counts[way] - 1, pl.ds(k * cut, cut)]
        grad[k * cut : (k + 1) * cut] = value

    go.finish()
    for step in range(1, SIDE):
        info_x(step).wait_send()
        info_y(step).wait_send()
        info_relay(step).wait_send()
        share(0, step).wait_send()
        share(1, step).wait_send()
        home(0, step, 0).wait_send()
        for f in range(SIDE):
            home(1, f, step).wait_send()
    for way, count in ((0, ups), (1, downs)):
        for step in range(count):
            gather(way, step).wait_send()
    for p in range(PASSES):
        for half in range(2):
            twin(p, half).wait_send()
            for step in range(1, SIDE):
                err_first(p, half, step).wait_send()
            for hop in range(1, SIDE):
                for late in range(1 if p else 0, 2):
                    err_second(p, half, hop, late).wait_send()
    for stage in range(stages):
        for step in range(1, stage_sizes[stage]):
            tell(stage, step).wait_send()
    for way in range(2):
        for step in range(ring_counts[way]):
            for k in range(CUTS):
                pass_on(way, step, k).wait_send()


def local(nz, tokens, targets, routes, route_logits, slot_order, seq_ids, w_gate, w_up, w_down):
    tok, feat = tokens.shape
    units = w_gate.shape[2]
    scale = float(tok * lax.axis_size("dp") * lax.axis_size("expert") // 8)
    width = feat // 2

    vmem = pl.BlockSpec(memory_space=pltpu.VMEM)
    dma = pltpu.SemaphoreType.DMA
    travel = [
        pltpu.VMEM((2, SIDE - 1, tok, width), BF16),
        pltpu.VMEM((2, SIDE, SIDE, CAP, width), BF16),
        pltpu.VMEM((2, SIDE, SIDE, CAP, width), BF16),
    ]
    travel_sems = [
        dma((2, SIDE - 1)), dma((2, SIDE - 1)), dma((2, SIDE, SIDE)), dma((2, SIDE, SIDE)),
    ]
    flops = 2 * EXPERTS * CAP * feat * units
    blocks = feat // LANES
    block = LANES // 2
    per = blocks // (2 * PASSES)
    mixed, grad, losses = pl.pallas_call(
        functools.partial(step_kernel, nz, scale),
        out_shape=(
            jax.ShapeDtypeStruct((tok, feat), BF16),
            jax.ShapeDtypeStruct((block, units), F32),
            jax.ShapeDtypeStruct((8, 2 * NSEQ), F32),
        ),
        in_specs=[vmem] * 9,
        out_specs=[vmem] * 3,
        scratch_shapes=[
            pltpu.VMEM((ROWS_INFO, tok), F32),
            pltpu.VMEM((SIDE, SIDE, ROWS_INFO, tok), F32),
            pltpu.VMEM((SIDE, SIDE * CAP, units), BF16),
            pltpu.VMEM((nz, 2, feat // (2 * nz), units), BF16),
            *travel,
            pltpu.VMEM((2, SIDE, SIDE, CAP, width), BF16),
            pltpu.VMEM((2, SIDE, SIDE, CAP, width), BF16),
            pltpu.VMEM((2, SIDE - 1, tok, width), BF16),
            pltpu.VMEM((2, SIDE - 1, tok, width), BF16),
            pltpu.VMEM((blocks, tok, LANES), BF16),
            pltpu.VMEM((PASSES, 2, SIDE - 1, per, tok, LANES), BF16),
            pltpu.VMEM((PASSES, 2, SIDE, SIDE, CAP, per * LANES), BF16),
            pltpu.VMEM((PASSES, 2, SIDE, SIDE, CAP, per * LANES), BF16),
            pltpu.VMEM((3, max(2 * SIDE, nz), 8, 2 * NSEQ), F32),
            pltpu.VMEM((blocks, 2, block, units), F32),
            pltpu.VMEM((blocks, block, units), F32),
            pltpu.VMEM((2, blocks // 2, block, units), F32),
            pltpu.VMEM((2, blocks // 2, block, units), F32),
            dma((3, SIDE - 1)), dma((3, SIDE - 1)),
            *travel_sems,
            dma((2, nz // 2 + 1)), dma((2, nz // 2 + 1)),
            dma((2, SIDE, SIDE)), dma((2, SIDE, SIDE)),
            dma((2, SIDE - 1)), dma((2, SIDE - 1)),
            dma((PASSES, 2, SIDE - 1)), dma((PASSES, 2, SIDE - 1)),
            dma((PASSES, 2, SIDE, 2)), dma((PASSES, 2, SIDE, 2)),
            dma((3, max(2 * SIDE, nz))), dma((3, max(2 * SIDE, nz))),
            dma((PASSES, 2)), dma((PASSES, 2)),
            dma((2, blocks // 2, CUTS)), dma((2, blocks // 2, CUTS)),
        ],
        compiler_params=pltpu.CompilerParams(
            collective_id=0, has_side_effects=True, vmem_limit_bytes=60 * 2**20
        ),
        cost_estimate=pl.CostEstimate(flops=4 * flops, bytes_accessed=8 * 2**20, transcendentals=0),
        name="robust_step",
    )(tokens, targets, routes.T, route_logits.T, slot_order.T, seq_ids[None, :], w_gate[0], w_up[0], w_down[:, 0])
    return (mixed, losses[0, :NSEQ], losses[1, :NSEQ], grad[:, None, :])


def solution(mesh):
    return jax.shard_map(
        functools.partial(local, mesh.shape["dp"] // 2),
        mesh=mesh,
        in_specs=(
            P(("dp", "expert"), None),
            P(("dp", "expert"), None),
            P(("dp", "expert"), None),
            P(("dp", "expert"), None),
            P(("dp", "expert"), None),
            P(("dp", "expert")),
            P("expert", None, None),
            P("expert", None, None),
            P("dp", "expert", None),
        ),
        out_specs=(P(("dp", "expert"), None), P(), P(), P("dp", "expert", None)),
        check_vma=False,
    )
```
